128 devices in a mesh: seq: 8 (over x_hi, z), doc: 16 (over x_lo, y, core).
Axes of the slice: x: 4 (x_hi: 2, x_lo: 2; x = x_hi * 2 + x_lo), y: 4, z: 4, core: 2. Of those that a mesh axis runs over, the one named last changes fastest.
Arguments:
- hidden_in: bfloat16 [16, 1024, 2880], P('doc', 'seq'), may hold values from -6 to 6
- queries: bfloat16 [16, 1024, 4096], P('doc', 'seq'), may hold values from -8 to 8
- key_heads: bfloat16 [16, 1024, 512], P('doc', 'seq'), may hold values from -8 to 8
- values: bfloat16 [16, 1024, 512], P('doc', 'seq'), may hold values from -6 to 6
- doc_lengths: int32 [16], P('doc'), may hold values from 1 to 1024, 10240 in all
- out_weight: bfloat16 [4096, 2880], P('seq'), may hold values from -0.75 to 0.75
- norm_gain: bfloat16 [2880], replicated, may hold values from 0.099609375 to 1.8984375
- router_weight: bfloat16 [2880, 64], replicated, may hold values from -0.109375 to 0.109375
- expert_ids: int32 [16, 1024, 4], P('doc', 'seq'), may hold values from 0 to 63, all different within a row; in each aligned block of 128 rows (0 to 127, 128 to 255, ..., all dimensions but the last counted through in order) at most 12 rows name the same one
- gate_weight: bfloat16 [128, 2880, 768], P(('seq', 'doc')), may hold values from -0.109375 to 0.109375
- up_weight: bfloat16 [128, 2880, 768], P(('seq', 'doc')), may hold values from -0.109375 to 0.109375
- down_weight: bfloat16 [128, 768, 2880], P(('seq', 'doc')), may hold values from -0.15625 to 0.15625
Outputs:
- layer_out: bfloat16 [16, 1024, 2880], P('doc', 'seq')
The draws below stay inside these ranges and needn't reach their ends.
Inputs may be any that keep to these rules, and one draw needn't show every extreme that they name: `doc_lengths`: the lengths sum to 10240, and the longest is 1024. `expert_ids`: each token names 4 different experts. Among the 128 positions that one device holds (aligned blocks of a document), no expert is named more than 12 times, and in some such block an expert is named exactly 12 times.
All inputs are finite; a program needn't handle non-finite values. No bound on the sum of `doc_lengths` on one device may be relied on, other than what follows from the above.
Results may differ from the reference program's by a relative error of at most 0.02.
Values may be sent and summed in bfloat16 or wider, within the bound.
No kernel may reach another device: no remote copies, remote signals or barrier semaphores. Data moves between devices by JAX's collectives and lax.ppermute only.
A program may use at most 128 MiB of HBM per device.

```python
import math
import jax
import jax.numpy as jnp
import numpy as np
from jax import lax

D = 2880
HEADS = 64
KVH = 8
HD = 64
FF = 1536
TOP = 4
TOK_DEV = 128
LEN = 1024
DOCS = 16
EXPERTS = 64
CAP = 12
N_SEQ = 8
N_DOC = 16


def attention_pair(key):
    query_seed = jax.random.fold_in(key, 101)
    keys_seed = jax.random.fold_in(key, 202)
    query_draw = jnp.clip(jax.random.normal(query_seed, (DOCS, LEN, HEADS, HD), jnp.float32), -6.0, 6.0)
    keys_draw = jnp.clip(jax.random.normal(keys_seed, (DOCS, LEN, KVH, HD), jnp.float32), -6.0, 6.0)
    return (query_draw.reshape(DOCS, LEN, HEADS * HD), keys_draw.reshape(DOCS, LEN, KVH * HD))


def draw_queries(key, part):
    return attention_pair(key)[0].astype(jnp.bfloat16)


def draw_key_heads(key, part):
    return attention_pair(key)[1].astype(jnp.bfloat16)


def shard_levels(stream_key, extent, split, smallest, top_value):
    def one(dim, parts):
        steps = jax.random.uniform(jax.random.fold_in(jax.random.fold_in(stream_key, 6), dim), (parts,), jnp.float32, smallest / len(split), top_value / len(split))
        return jnp.repeat(jnp.exp(steps), extent[dim] // parts).reshape((-1,) + (1,) * (len(extent) - dim - 1))

    factor_of = one(*split[0])
    for cut in split[1:]:
        factor_of = factor_of * one(*cut)
    return factor_of


def profile(count, total, limit, lean):
    weights = [(1 << 20) // math.isqrt(grade ** lean) + 1 for grade in range(2, count + 1)]
    rest, counts = total - limit - (count - 1), [1] * (count - 1)
    while rest > 0:
        candidates = [i for i in range(count - 1) if counts[i] < limit]
        pool, remaining = sum([weights[i] for i in candidates]), rest
        for i in candidates:
            addition = min(limit - counts[i], max(1, remaining * weights[i] // pool), rest)
            counts[i] = counts[i] + addition
            rest = rest - addition
    return np.array([limit] + counts)


def uneven_parts(stream_key, amount, total, reach, lean):
    if amount == 2:
        one = jax.random.randint(stream_key, (), max(1, total - reach), min(reach, total - 1) + 1)
        return jnp.stack([one, total - one])
    tallies = jnp.asarray(profile(amount, total, reach, lean), jnp.int32)
    pairs = (amount - 1) // 2
    source_of, receiver = tallies[1:1 + 2 * pairs:2], tallies[2:2 + 2 * pairs:2]
    room = jnp.minimum(source_of - 1, reach - receiver)
    shifted = jax.random.randint(jax.random.fold_in(stream_key, 1), (pairs,), 0, 1 << 20) % (room + 1)
    tallies = tallies.at[1:1 + 2 * pairs:2].set(source_of - shifted).at[2:2 + 2 * pairs:2].set(receiver + shifted)
    return tallies[jax.random.permutation(jax.random.fold_in(stream_key, 2), amount)]


def shared_out(key, own, number, rows, count, top, most, skew):
    ranking = jax.random.permutation(key, count)
    heavy_load, usual = portions_of(count, rows * top, most, skew, True), portions_of(count, rows * top, most, skew, False)
    places = jnp.arange(count)

    def named(tallies, offset_by):
        used = int((tallies > 0).sum())
        fixed = max(1, used // 4)
        passed = fixed + (places - fixed + offset_by * (used - fixed)) % max(1, count - fixed)
        return jnp.zeros((count,), jnp.int32).at[ranking[jnp.where(places < fixed, places, passed)]].set(jnp.asarray(tallies, jnp.int32))

    tallies = jnp.where(number % 4 == 0, named(heavy_load, number // 4), named(usual, number - number // 4 - 1))
    mixed = jax.random.permutation(jax.random.fold_in(own, 3), count)
    donor, sink = mixed[0:count // 2 * 2:2], mixed[1:count // 2 * 2:2]
    room = jnp.minimum(tallies[donor] - 1, most - tallies[sink]) // 2
    room = jnp.where((donor == ranking[0]) | (sink == ranking[0]) | (tallies[sink] == 0), 0, jnp.maximum(room, 0))
    passed = jax.random.randint(jax.random.fold_in(own, 4), (count // 2,), 0, 1 << 20) % (room + 1)
    tallies = tallies.at[donor].add(-passed).at[sink].add(passed)
    members = jnp.searchsorted(jnp.cumsum(tallies), jnp.arange(rows * top), side="right").astype(jnp.int32)
    grid = members.reshape(top, rows).T
    grid = grid[jax.random.permutation(jax.random.fold_in(own, 1), rows)]
    offset_by = jax.random.randint(jax.random.fold_in(own, 2), (rows, 1), 0, top)
    return jnp.take_along_axis(grid, (jnp.arange(top)[None, :] + offset_by) % top, axis=1)


def portions_of(count, total, most, lean, full):
    weights = [(1 << 20) // math.isqrt(rank ** lean) + 1 for rank in range(1, count + 1)]
    largest = most if full else min(most, max(-(-total // count), total * weights[0] // sum(weights)))
    least = 1 if total - largest >= count - 1 else 0
    counts, spare = [largest] + [least] * (count - 1), total - largest - least * (count - 1)
    while spare > 0:
        candidates = [i for i in range(1, count) if counts[i] < largest] or [i for i in range(1, count) if counts[i] < most]
        whole, remaining = sum([weights[i] for i in candidates]), spare
        for i in candidates:
            more = min(most - counts[i], max(1, remaining * weights[i] // whole), spare)
            counts[i] = counts[i] + more
            spare = spare - more
    return np.array(counts)


def scatter_about(key, dims, deviation, reach, shards=(), kind=jnp.bfloat16):
    entries = deviation * jax.random.normal(key, dims, jnp.float32)
    if shards:
        entries = entries * shard_levels(key, dims, shards, -0.22, 0.18)
    return jnp.clip(entries, -reach, reach).astype(kind)


def setup_inputs(seed: int = 0) -> dict:
    key_list = jax.random.split(jax.random.key(seed), 13)
    hidden_in = scatter_about(key_list[0], (DOCS, LEN, D), 1.0, 6.0, ((0, 16), (1, 8)))
    queries = draw_queries(jax.random.fold_in(key_list[12], 71), 0)
    key_heads = draw_key_heads(jax.random.fold_in(key_list[12], 71), 0)
    values = scatter_about(key_list[3], (DOCS, LEN, KVH * HD), 1.0, 6.0, ((0, 16), (1, 8)))
    doc_lengths = uneven_parts(key_list[4], DOCS, DOCS * LEN * 5 // 8, LEN, 1).astype(jnp.int32)
    out_weight = scatter_about(key_list[5], (HEADS * HD, D), HD ** -0.5, 0.75, ((0, 8),))
    norm_gain = jnp.clip(1.0 + 0.18 * jax.random.normal(key_list[6], (D,), jnp.float32), 0.099609375, 1.8984375).astype(jnp.bfloat16)
    router_weight = scatter_about(key_list[7], (D, EXPERTS), D ** -0.5, 0.109375)
    expert_ids_keys = jax.random.split(jax.random.fold_in(key_list[8], 1), DOCS * LEN // TOK_DEV)
    expert_ids_turns = jax.random.permutation(jax.random.fold_in(key_list[8], 3), DOCS * LEN // TOK_DEV)
    expert_ids = jax.vmap(lambda own, number: shared_out(jax.random.fold_in(key_list[8], 2), own, number, TOK_DEV, EXPERTS, TOP, CAP, 2))(expert_ids_keys, expert_ids_turns).reshape((DOCS, LEN, TOP))
    gate_weight = scatter_about(key_list[9], (2 * EXPERTS, D, FF // 2), D ** -0.5, 0.109375, ((0, 128),))
    up_weight = scatter_about(key_list[10], (2 * EXPERTS, D, FF // 2), D ** -0.5, 0.109375, ((0, 128),))
    down_weight = scatter_about(key_list[11], (2 * EXPERTS, FF // 2, D), FF ** -0.5, 0.15625, ((0, 128),))
    return {"hidden_in": hidden_in, "queries": queries, "key_heads": key_heads, "values": values, "doc_lengths": doc_lengths, "out_weight": out_weight, "norm_gain": norm_gain, "router_weight": router_weight, "expert_ids": expert_ids, "gate_weight": gate_weight, "up_weight": up_weight, "down_weight": down_weight}


negative_fill = -1e+30
swiglu_alpha = 1.702
norm_eps = 1e-05

def rounded(tensor_in):
    return lax.optimization_barrier(tensor_in.astype(jnp.bfloat16))

def attend_doc(inputs):
    doc_queries, doc_keys, doc_values, doc_length = inputs
    group_size = HEADS // KVH
    query_heads = doc_queries.reshape(LEN, KVH, group_size, HD).transpose(1, 0, 2, 3)
    key_heads = doc_keys.reshape(LEN, KVH, HD).transpose(1, 0, 2)
    value_heads = doc_values.reshape(LEN, KVH, HD).transpose(1, 0, 2)
    position = jnp.arange(LEN, dtype=jnp.int32)
    allowed = (position[None, :] <= position[:, None]) & (position[None, :] < doc_length)

    def one_head(triple_in):
        head_query, head_key, head_value = triple_in
        scores = jnp.einsum('qgd,jd->gqj', head_query.astype(jnp.float32), head_key.astype(jnp.float32)) * HD ** (-0.5)
        scores = jnp.where(allowed[None], scores, negative_fill)
        row_top = lax.optimization_barrier(jnp.max(scores, axis=-1, keepdims=True))
        weights = jnp.where(allowed[None], jnp.exp(scores - row_top), 0.0)
        row_total = lax.optimization_barrier(jnp.sum(weights, axis=-1))
        mixed = jnp.einsum('gqj,jd->gqd', rounded(weights).astype(jnp.float32), head_value.astype(jnp.float32))
        return (mixed / row_total[..., None]).astype(jnp.bfloat16)
    heads_out = lax.map(one_head, (query_heads, key_heads, value_heads))
    return heads_out.transpose(2, 0, 1, 3).reshape(LEN, HEADS * HD)

def reference(hidden_in, queries, key_heads, values, doc_lengths, out_weight, norm_gain, router_weight, expert_ids, gate_weight, up_weight, down_weight):
    token_count = DOCS * LEN
    attended = lax.map(attend_doc, (queries, key_heads, values, doc_lengths))
    attended = attended.reshape(token_count, HEADS * HD)
    group_width = HEADS * HD // N_SEQ
    attention_sum = jnp.zeros((token_count, D), jnp.float32)
    for group_idx in range(N_SEQ):
        lower = group_idx * group_width
        term = jnp.dot(attended[:, lower:lower + group_width], out_weight[lower:lower + group_width], preferred_element_type=jnp.float32)
        attention_sum = attention_sum + rounded(term).astype(jnp.float32)
    residual = rounded(hidden_in.reshape(token_count, D).astype(jnp.float32) + attention_sum).astype(jnp.float32)
    mean_square = lax.optimization_barrier(jnp.mean(residual * residual, axis=-1, keepdims=True))
    normed = (residual * lax.rsqrt(mean_square + norm_eps) * norm_gain.astype(jnp.float32)).astype(jnp.bfloat16)
    logits = jnp.dot(normed, router_weight, preferred_element_type=jnp.float32)
    chosen_ids = expert_ids.reshape(token_count, TOP)
    expert_range = jnp.arange(EXPERTS, dtype=jnp.int32)
    matches = chosen_ids[:, :, None] == expert_range[None, None, :]
    chosen_logits = lax.optimization_barrier(jnp.sum(jnp.where(matches, logits[:, None, :], 0.0), axis=-1))
    raised = jnp.exp(chosen_logits)
    route_share = raised / lax.optimization_barrier(jnp.sum(raised, axis=-1, keepdims=True))
    flat_ids = chosen_ids.reshape(-1)
    one_hot = (flat_ids[:, None] == expert_range[None, :]).astype(jnp.int32)
    slot_rank = (lax.optimization_barrier(jnp.sum(jnp.cumsum(one_hot, axis=0) * one_hot, axis=1)) - 1).astype(jnp.int32)
    room_all = N_SEQ * N_DOC * CAP
    pair_count = token_count * TOP
    slot_table = jnp.full((EXPERTS, room_all), pair_count, jnp.int32).at[flat_ids, slot_rank].set(jnp.arange(pair_count, dtype=jnp.int32))
    padded = jnp.concatenate([normed, jnp.zeros((1, D), jnp.bfloat16)], axis=0)
    share_padded = jnp.concatenate([route_share.reshape(-1), jnp.zeros((1,), jnp.float32)])
    gate_pairs = gate_weight.reshape(EXPERTS, 2, D, FF // 2)
    up_pairs = up_weight.reshape(EXPERTS, 2, D, FF // 2)
    down_pairs = down_weight.reshape(EXPERTS, 2, FF // 2, D)

    def one_expert(accum_out, expert_in):
        slots, gate_pair, up_pair, down_pair = expert_in
        token_rows = (slots // TOP).astype(jnp.int32)
        picked_rows = padded[token_rows]
        pieces = []
        for half_idx in range(2):
            gate_val = jnp.dot(picked_rows, gate_pair[half_idx], preferred_element_type=jnp.float32)
            up_val = jnp.dot(picked_rows, up_pair[half_idx], preferred_element_type=jnp.float32)
            active = (gate_val * jax.nn.sigmoid(swiglu_alpha * gate_val) * (up_val + 1.0)).astype(jnp.bfloat16)
            pieces.append(rounded(jnp.dot(active, down_pair[half_idx], preferred_element_type=jnp.float32)).astype(jnp.float32))
        expert_out = rounded(pieces[0] + pieces[1]).astype(jnp.float32)
        accum_out = accum_out.at[token_rows].add(share_padded[slots][:, None] * expert_out)
        return (accum_out, None)
    accum_out, _ = lax.scan(one_expert, jnp.zeros((token_count + 1, D), jnp.float32), (slot_table, gate_pairs, up_pairs, down_pairs))
    layer_out = (residual + accum_out[:token_count]).astype(jnp.bfloat16)
    return layer_out.reshape(DOCS, LEN, D)
```

```python
import functools
import jax
import jax.numpy as jnp
from jax import lax
from jax.experimental import pallas as pl
from jax.experimental.pallas import tpu as pltpu
from jax.sharding import Mesh, PartitionSpec as P

HEADS = 64
KVH = 8
HD = 64
TOP = 4
CAP = 12
EXPERTS = 64
TOK = 128
D = 2880
FF = 768
GW = 512
HALF = 1440
WIDE = 1536
SECOND = D - WIDE
SKIP = HALF - SECOND
PAIR_ROWS = 2 * CAP
ROWS = EXPERTS * PAIR_ROWS

negative_fill = -1e30
swiglu_alpha = 1.702
norm_eps = 1e-05
exp_scale = HD ** (-0.5) * 1.4426950408889634

f32 = jnp.float32
bf16 = jnp.bfloat16
VMEM_SPEC = pl.BlockSpec(memory_space=pltpu.VMEM)
SMEM_SPEC = pl.BlockSpec(memory_space=pltpu.SMEM)
NT = (((1,), (1,)), ((), ()))
TN = (((0,), (0,)), ((), ()))


def attention_kernel(info, qkv, own_w, first_w, second_w, out, keys, vals, att):
    upper = info[0]
    core = info[1]
    doc_len = info[2]
    lane = lax.broadcasted_iota(jnp.int32, (512, 128), 1)
    low = lane < 64
    one = jnp.ones((512, 128), f32)
    for side in range(2):
        base = 1280 - 256 * side
        rows = pl.ds(512 * side, 512)
        kk = qkv[:, base : base + 128].astype(f32)
        vv = qkv[:, base + 128 : base + 256].astype(f32)
        kr = pltpu.roll(kk, 64, 1)
        vr = pltpu.roll(vv, 64, 1)
        for a in range(2):
            for par in range(2):
                keep = low if par == 0 else ~low
                k_src = kk if a == par else kr
                v_src = vv if a == par else vr
                slot = 2 * a + par
                keys[slot, rows, :] = jnp.where(keep, k_src, 0.0).astype(bf16)
                vals[slot, rows, 0:128] = jnp.where(keep, v_src, 0.0).astype(bf16)
                vals[slot, rows, 128:256] = jnp.where(keep, one, 0.0).astype(bf16)

    row_id = lax.broadcasted_iota(jnp.int32, (128, 128), 0)
    col_id = lax.broadcasted_iota(jnp.int32, (128, 128), 1)

    def block(a, pair, i, with_other):
        nk = (i + 1) * 128 + (512 if with_other else 0)
        start = 0 if with_other else 512
        q_rows = slice(i * 128, (i + 1) * 128)
        q_base = pl.multiple_of(a * 512 + pair * 256, 256)
        q_tiles = [
            qkv[q_rows, pl.ds(pl.multiple_of(q_base + 128 * t, 128), 128)] for t in range(2)
        ]
        q_stack = jnp.concatenate(q_tiles, axis=0)
        position = lax.broadcasted_iota(jnp.int32, (1, nk), 1)
        length_bias = jnp.where(position < doc_len, 0.0, negative_fill)
        query = row_id + (nk - 128)
        diag = jnp.where(col_id <= row_id, 0.0, negative_fill) + length_bias[:, nk - 128 :]
        diag = jnp.concatenate([diag] * 2, axis=0)
        total = None
        for par in range(2):
            k_blk = keys[2 * a + par, start : start + nk, :]
            scores = lax.dot_general(q_stack, k_blk, NT, preferred_element_type=f32)
            last = scores[:, nk - 128 :] + diag
            if nk > 128:
                scores = jnp.concatenate(
                    [scores[:, : nk - 128] + length_bias[:, : nk - 128], last], axis=1
                )
            else:
                scores = last
            top = jnp.max(scores, axis=1, keepdims=True)
            weights = jnp.exp2((scores - top) * exp_scale).astype(bf16)
            part = jnp.dot(
                weights, vals[2 * a + par, start : start + nk, :], preferred_element_type=f32
            )
            total = part if total is None else total + part
        result = (total[:, 0:128] / total[:, 128:256]).astype(bf16)
        for t in range(2):
            att[q_rows, pl.ds(pl.multiple_of(q_base + 128 * t, 128), 128)] = result[
                128 * t : 128 * (t + 1)
            ]

    def all_blocks(with_other):
        def body(n, carry):
            for i in range(4):
                block(n // 2, n % 2, i, with_other)
            return carry

        lax.fori_loop(0, 4, body, 0)

    pl.when(upper == 1)(lambda: all_blocks(True))
    pl.when(upper == 0)(lambda: all_blocks(False))

    own = att[:, pl.ds(pl.multiple_of(upper * 512, 512), 512)]
    other = (1 - upper) * 512
    first = att[:, pl.ds(pl.multiple_of(other + core * 256, 256), 256)]
    second = att[:, pl.ds(pl.multiple_of(other + (1 - core) * 256, 256), 256)]
    for lo in range(0, D, 512):
        hi = min(lo + 512, D)
        term = jnp.dot(own, own_w[:, lo:hi], preferred_element_type=f32)
        term += jnp.dot(first, first_w[:, lo:hi], preferred_element_type=f32)
        term += jnp.dot(second, second_w[:, lo:hi], preferred_element_type=f32)
        out[:, lo:hi] = term.astype(bf16)


def norm_kernel(info, parts, hidden, gain, router, ids, residual_out, own_out, send_out, share_out):
    core = info[1]
    acc = hidden[...].astype(f32)
    for z in range(4):
        acc = acc + parts[z].astype(f32)
    rounded = acc.astype(bf16)
    residual_out[...] = rounded
    res = rounded.astype(f32)
    mean_square = jnp.sum(res * res, axis=1, keepdims=True) * (1.0 / D)
    scaled = res * lax.rsqrt(mean_square + norm_eps) * gain[...].astype(f32)
    normed = scaled.astype(bf16)
    logits = lax.dot_general(router[...], normed, NT, preferred_element_type=f32)
    expert = lax.broadcasted_iota(jnp.int32, (EXPERTS, TOK), 0)
    named = expert == ids[0:1, :]
    for k in range(1, TOP):
        named = named | (expert == ids[k : k + 1, :])
    raised = jnp.where(named, jnp.exp(logits), 0.0)
    share_out[...] = raised / jnp.sum(raised, axis=0, keepdims=True)
    lane = lax.broadcasted_iota(jnp.int32, (TOK, WIDE), 1)
    half0 = jnp.where(lane < HALF, scaled[:, :WIDE], 0.0)
    half1 = jnp.where(lane >= SKIP, scaled[:, SECOND:], 0.0)
    own_out[...] = jnp.where(core == 0, half0, half1).astype(bf16)
    send_out[...] = jnp.where(core == 0, half1, half0).astype(bf16)


def slots_of(ids, offset):
    expert = lax.broadcasted_iota(jnp.int32, (EXPERTS, TOK), 0)
    named = expert == ids[0:1, :]
    for k in range(1, TOP):
        named = named | (expert == ids[k : k + 1, :])
    before = lax.broadcasted_iota(jnp.int32, (TOK, TOK), 0) < lax.broadcasted_iota(
        jnp.int32, (TOK, TOK), 1
    )
    rank = jnp.dot(
        named.astype(f32).astype(bf16), before.astype(f32).astype(bf16), preferred_element_type=f32
    )
    return jnp.where(named, rank + offset, -1.0)


def slot_scratch(core, own_ids, other_ids, slots):
    start = (core * CAP).astype(f32)
    slots[:, 0:TOK] = slots_of(own_ids, start)
    slots[:, TOK : 2 * TOK] = slots_of(other_ids, CAP - start)


def hits(slots, first, count):
    block = slots[pl.ds(first, count), :]
    place = lax.broadcasted_iota(jnp.int32, (count, PAIR_ROWS, 2 * TOK), 1).astype(f32)
    return block[:, None, :] == place


EXPERT_BLOCK = 16
ROW_BLOCK = EXPERT_BLOCK * PAIR_ROWS


def dispatch_kernel(info, own, other, own_ids, other_ids, out, slots):
    slot_scratch(info[1], own_ids, other_ids, slots)
    tokens = jnp.concatenate([own[...], other[...]], axis=0)

    def body(n, carry):
        hit = hits(slots, pl.multiple_of(n * EXPERT_BLOCK, EXPERT_BLOCK), EXPERT_BLOCK)
        pick = jnp.where(hit, 1.0, 0.0).reshape(ROW_BLOCK, 2 * TOK).astype(bf16)
        out[pl.ds(pl.multiple_of(n * ROW_BLOCK, ROW_BLOCK), ROW_BLOCK), :] = jnp.dot(
            pick, tokens, preferred_element_type=f32
        ).astype(bf16)
        return carry

    lax.fori_loop(0, EXPERTS // EXPERT_BLOCK, body, 0)


def combine_kernel(info, rows, own_ids, other_ids, own_share, other_share, own_out, other_out, slots, share):
    slot_scratch(info[1], own_ids, other_ids, slots)
    share[:, 0:TOK] = own_share[...]
    share[:, TOK : 2 * TOK] = other_share[...]
    own_out[...] = jnp.zeros_like(own_out)
    other_out[...] = jnp.zeros_like(other_out)

    def body(n, carry):
        first = pl.multiple_of(n * EXPERT_BLOCK, EXPERT_BLOCK)
        hit = hits(slots, first, EXPERT_BLOCK)
        factor = share[pl.ds(first, EXPERT_BLOCK), :][:, None, :]
        factor = jnp.where(hit, factor, 0.0).reshape(ROW_BLOCK, 2 * TOK)
        high = factor.astype(bf16)
        rest = (factor - high.astype(f32)).astype(bf16)
        block = rows[pl.ds(pl.multiple_of(n * ROW_BLOCK, ROW_BLOCK), ROW_BLOCK), :]
        mix = lax.dot_general(high, block, TN, preferred_element_type=f32)
        mix += lax.dot_general(rest, block, TN, preferred_element_type=f32)
        own_out[...] += mix[:TOK]
        other_out[...] += mix[TOK:]
        return carry

    lax.fori_loop(0, EXPERTS // EXPERT_BLOCK, body, 0)


def expert_kernel(info, own, other, gate_w, up_w, down_w, keep_out, send_out, down):
    core = info[1]

    @pl.when(pl.program_id(0) == 0)
    def _():
        down[0] = down_w[:, 0:WIDE]
        down[1] = down_w[:, SECOND:D]

    own_rows = pl.ds(pl.multiple_of(core * SECOND, 64), WIDE)
    other_rows = pl.ds(pl.multiple_of((1 - core) * SECOND, 64), WIDE)
    x_own = own[...]
    x_other = other[...]
    gate = jnp.dot(x_own, gate_w[own_rows, :], preferred_element_type=f32)
    gate += jnp.dot(x_other, gate_w[other_rows, :], preferred_element_type=f32)
    up = jnp.dot(x_own, up_w[own_rows, :], preferred_element_type=f32)
    up += jnp.dot(x_other, up_w[other_rows, :], preferred_element_type=f32)
    active = (gate * jax.nn.sigmoid(swiglu_alpha * gate) * (up + 1.0)).astype(bf16)
    keep_out[...] = jnp.dot(active, down[core], preferred_element_type=f32).astype(bf16)
    send_out[...] = jnp.dot(active, down[1 - core], preferred_element_type=f32).astype(bf16)


def params(mib):
    return pltpu.CompilerParams(vmem_limit_bytes=mib << 20)


def final_kernel(info, residual, own, other, out):
    core = info[1]
    first = jnp.where(core == 0, own[...], other[...])
    second = jnp.where(core == 0, other[...], own[...])
    lane = lax.broadcasted_iota(jnp.int32, (TOK, D), 1)
    blank = jnp.zeros((TOK, SECOND), f32)
    low = jnp.concatenate([first, blank], axis=1)
    high = jnp.concatenate([blank, second], axis=1)
    mix = jnp.where(lane < HALF, low, high)
    out[...] = (residual[...].astype(f32) + mix).astype(bf16)


def local(
    hidden_in,
    queries,
    key_heads,
    values,
    doc_lengths,
    out_weight,
    norm_gain,
    router_weight,
    expert_ids,
    gate_weight,
    up_weight,
    down_weight,
):
    upper = lax.axis_index("xh")
    core = lax.axis_index("c")
    info = jnp.stack([upper, core, doc_lengths[0]]).astype(jnp.int32)
    swap = [(0, 1), (1, 0)]

    half_rows = lax.dynamic_slice_in_dim(out_weight, core * 256, 256, axis=0)
    first_w = lax.ppermute(half_rows, ("xh", "xl"), [(0, 3), (3, 0), (1, 2), (2, 1)])
    second_w = lax.ppermute(first_w, "c", swap)

    ids = expert_ids[0].T
    other_ids = lax.ppermute(ids, "c", swap)

    kv = jnp.concatenate(
        [
            key_heads[0].reshape(TOK, 2, 4, HD).transpose(2, 0, 1, 3).reshape(4, TOK, 128),
            values[0].reshape(TOK, 2, 4, HD).transpose(2, 0, 1, 3).reshape(4, TOK, 128),
        ],
        axis=2,
    )
    lower_kv = lax.ppermute(kv, "xh", [(0, 1)])
    q = queries[0].reshape(TOK, 2, 4, 512).transpose(2, 0, 1, 3).reshape(4, TOK, 1024)
    qkv = lax.all_to_all(
        jnp.concatenate([q, kv, lower_kv], axis=2), "z", split_axis=0, concat_axis=0, tiled=True
    ).reshape(512, 1536)

    partial = pl.pallas_call(
        attention_kernel,
        out_shape=jax.ShapeDtypeStruct((512, D), bf16),
        in_specs=[SMEM_SPEC] + [VMEM_SPEC] * 4,
        out_specs=VMEM_SPEC,
        scratch_shapes=[
            pltpu.VMEM((4, 1024, 128), bf16),
            pltpu.VMEM((4, 1024, 256), bf16),
            pltpu.VMEM((512, 1024), bf16),
        ],
        compiler_params=params(48),
    )(info, qkv, out_weight, first_w, second_w)
    parts = lax.all_to_all(
        partial.reshape(4, TOK, D), "z", split_axis=0, concat_axis=0, tiled=True
    )

    residual, own_half, send_half, share = pl.pallas_call(
        norm_kernel,
        out_shape=[
            jax.ShapeDtypeStruct((TOK, D), bf16),
            jax.ShapeDtypeStruct((TOK, WIDE), bf16),
            jax.ShapeDtypeStruct((TOK, WIDE), bf16),
            jax.ShapeDtypeStruct((EXPERTS, TOK), f32),
        ],
        in_specs=[SMEM_SPEC] + [VMEM_SPEC] * 5,
        out_specs=[VMEM_SPEC] * 4,
        compiler_params=params(40),
    )(info, parts, hidden_in[0], norm_gain[None], router_weight.T, ids)
    other_half = lax.ppermute(send_half, "c", swap)
    other_share = lax.ppermute(share, "c", swap)

    outgoing = pl.pallas_call(
        dispatch_kernel,
        out_shape=jax.ShapeDtypeStruct((ROWS, WIDE), bf16),
        in_specs=[SMEM_SPEC] + [VMEM_SPEC] * 4,
        out_specs=VMEM_SPEC,
        scratch_shapes=[pltpu.VMEM((EXPERTS, 2 * TOK), f32)],
        compiler_params=params(40),
    )(info, own_half, other_half, ids, other_ids)
    chips = ("xh", "z", "xl", "y")
    arrived = lax.all_to_all(
        outgoing.reshape(EXPERTS, PAIR_ROWS, WIDE), chips, split_axis=0, concat_axis=0, tiled=True
    ).reshape(ROWS, WIDE)
    arrived_other = lax.ppermute(arrived, "c", swap)

    step = 256
    keep, send = pl.pallas_call(
        expert_kernel,
        grid=(ROWS // step,),
        out_shape=[jax.ShapeDtypeStruct((ROWS, WIDE), bf16)] * 2,
        in_specs=[
            SMEM_SPEC,
            pl.BlockSpec((step, WIDE), lambda i: (i, 0)),
            pl.BlockSpec((step, WIDE), lambda i: (i, 0)),
            VMEM_SPEC,
            VMEM_SPEC,
            VMEM_SPEC,
        ],
        out_specs=[pl.BlockSpec((step, WIDE), lambda i: (i, 0))] * 2,
        scratch_shapes=[pltpu.VMEM((2, FF, WIDE), bf16)],
        compiler_params=params(52),
    )(info, arrived, arrived_other, gate_weight[0], up_weight[0], down_weight[0])
    sent = lax.ppermute(send, "c", swap)
    expert_out = (keep.astype(f32) + sent.astype(f32)).astype(bf16)

    returned = lax.all_to_all(
        expert_out.reshape(EXPERTS, PAIR_ROWS, WIDE), chips, split_axis=0, concat_axis=0, tiled=True
    ).reshape(ROWS, WIDE)
    own_mix, send_mix = pl.pallas_call(
        combine_kernel,
        out_shape=[jax.ShapeDtypeStruct((TOK, WIDE), f32)] * 2,
        in_specs=[SMEM_SPEC] + [VMEM_SPEC] * 5,
        out_specs=[VMEM_SPEC] * 2,
        scratch_shapes=[pltpu.VMEM((EXPERTS, 2 * TOK), f32)] * 2,
        compiler_params=params(40),
    )(info, returned, ids, other_ids, share, other_share)
    other_mix = lax.ppermute(send_mix, "c", swap)
    layer_out = pl.pallas_call(
        final_kernel,
        out_shape=jax.ShapeDtypeStruct((TOK, D), bf16),
        in_specs=[SMEM_SPEC] + [VMEM_SPEC] * 3,
        out_specs=VMEM_SPEC,
        compiler_params=params(40),
    )(info, residual, own_mix, other_mix)
    return layer_out[None]


def solution(mesh):
    split_mesh = Mesh(mesh.devices.reshape(2, 4, 2, 4, 2), ("xh", "z", "xl", "y", "c"))
    seq = ("xh", "z")
    doc = ("xl", "y", "c")
    in_specs = (
        P(doc, seq, None),
        P(doc, seq, None),
        P(doc, seq, None),
        P(doc, seq, None),
        P(doc),
        P(seq, None),
        P(),
        P(),
        P(doc, seq, None),
        P(seq + doc, None, None),
        P(seq + doc, None, None),
        P(seq + doc, None, None),
    )
    return jax.shard_map(
        local,
        mesh=split_mesh,
        in_specs=in_specs,
        out_specs=P(doc, seq, None),
        check_vma=False,
    )
```

```python
import jax
import jax.numpy as jnp
from jax import lax
from jax.experimental import pallas as pl
from jax.experimental.pallas import tpu as pltpu
from jax.sharding import Mesh, PartitionSpec as P

HD = 64
TOP = 4
EXPERTS = 64
TOK = 128
D = 2880
FF = 768
HALF = D // 2
WIDE = 1536
CHUNKS = 3
SLOTS = 4
PAIR_SLOTS = 2 * SLOTS
ROWS = EXPERTS * PAIR_SLOTS
PART = 480

negative_fill = -1e30
swiglu_alpha = 1.702
norm_eps = 1e-05
exp_scale = HD ** (-0.5) * 1.4426950408889634

f32 = jnp.float32
bf16 = jnp.bfloat16
VMEM_SPEC = pl.BlockSpec(memory_space=pltpu.VMEM)
SMEM_SPEC = pl.BlockSpec(memory_space=pltpu.SMEM)
NT = (((1,), (1,)), ((), ()))


def prepare_kernel(queries, key_heads, values, lower_keys, lower_values, out):
    lane = lax.broadcasted_iota(jnp.int32, (TOK, 128), 1)
    for z in range(4):
        out[z, :, 0:512] = queries[:, z * 512 : z * 512 + 512]
        out[z, :, 512:1024] = queries[:, 2048 + z * 512 : 2560 + z * 512]
        tile = (z // 2) * 128
        for n, ref in enumerate((key_heads, values, lower_keys, lower_values)):
            first = ref[:, tile : tile + 128].astype(f32)
            second = ref[:, 256 + tile : 384 + tile].astype(f32)
            if z % 2 == 0:
                second = pltpu.roll(second, 64, 1)
            else:
                first = pltpu.roll(first, 64, 1)
            out[z, :, 1024 + 128 * n : 1152 + 128 * n] = jnp.where(
                lane < 64, first, second
            ).astype(bf16)


def attention_kernel(info, qkv, att, keys, vals):
    upper = info[0]
    doc_len = info[2]
    lane = lax.broadcasted_iota(jnp.int32, (512, 128), 1)
    low = lane < 64
    one = jnp.ones((512, 128), f32)
    for side in range(2):
        base = 1280 - 256 * side
        rows = pl.ds(512 * side, 512)
        kk = qkv[:, base : base + 128].astype(f32)
        vv = qkv[:, base + 128 : base + 256].astype(f32)
        kr = pltpu.roll(kk, 64, 1)
        vr = pltpu.roll(vv, 64, 1)
        for a in range(2):
            for par in range(2):
                keep = low if par == 0 else ~low
                k_src = kk if a == par else kr
                v_src = vv if a == par else vr
                slot = 2 * a + par
                keys[slot, rows, :] = jnp.where(keep, k_src, 0.0).astype(bf16)
                vals[slot, rows, 0:128] = jnp.where(keep, v_src, 0.0).astype(bf16)
                vals[slot, rows, 128:256] = jnp.where(keep, one, 0.0).astype(bf16)

    row_id = lax.broadcasted_iota(jnp.int32, (128, 128), 0)
    col_id = lax.broadcasted_iota(jnp.int32, (128, 128), 1)

    def block(a, pair, i, with_other):
        nk = (i + 1) * 128 + (512 if with_other else 0)
        start = 0 if with_other else 512
        q_rows = slice(i * 128, (i + 1) * 128)
        q_base = pl.multiple_of(a * 512 + pair * 256, 256)
        q_tiles = [
            qkv[q_rows, pl.ds(pl.multiple_of(q_base + 128 * t, 128), 128)] for t in range(2)
        ]
        q_stack = jnp.concatenate(q_tiles, axis=0)
        position = lax.broadcasted_iota(jnp.int32, (1, nk), 1)
        length_bias = jnp.where(position < doc_len, 0.0, negative_fill)
        query = row_id + (nk - 128)
        diag = jnp.where(col_id <= row_id, 0.0, negative_fill) + length_bias[:, nk - 128 :]
        diag = jnp.concatenate([diag] * 2, axis=0)
        total = None
        for par in range(2):
            k_blk = keys[2 * a + par, start : start + nk, :]
            scores = lax.dot_general(q_stack, k_blk, NT, preferred_element_type=f32)
            last = scores[:, nk - 128 :] + diag
            if nk > 128:
                scores = jnp.concatenate(
                    [scores[:, : nk - 128] + length_bias[:, : nk - 128], last], axis=1
                )
            else:
                scores = last
            top = jnp.max(scores, axis=1, keepdims=True)
            weights = jnp.exp2((scores - top) * exp_scale).astype(bf16)
            part = jnp.dot(
                weights, vals[2 * a + par, start : start + nk, :], preferred_element_type=f32
            )
            total = part if total is None else total + part
        result = (total[:, 0:128] / total[:, 128:256]).astype(bf16)
        for t in range(2):
            att[q_rows, pl.ds(pl.multiple_of(q_base + 128 * t, 128), 128)] = result[
                128 * t : 128 * (t + 1)
            ]

    def all_blocks(with_other):
        def body(n, carry):
            for i in range(4):
                block(n // 2, n % 2, i, with_other)
            return carry

        lax.fori_loop(0, 4, body, 0)

    pl.when(upper == 1)(lambda: all_blocks(True))
    pl.when(upper == 0)(lambda: all_blocks(False))


def project_kernel(info, att, own_w, first_w, second_w, out):
    upper = info[0]
    core = info[1]
    own = att[:, pl.ds(pl.multiple_of(upper * 512, 512), 512)]
    other = att[:, pl.ds(pl.multiple_of((1 - upper) * 512, 512), 512)]
    for half, far_w in ((core, first_w), (1 - core, second_w)):
        for lo in range(0, HALF, PART):
            rows = pl.ds(pl.multiple_of(half * HALF + lo, 32), PART)
            term = lax.dot_general(own_w[rows, :], own, NT, preferred_element_type=f32)
            term += lax.dot_general(
                far_w[lo : lo + PART, :], other, NT, preferred_element_type=f32
            )
            term = term.astype(bf16)
            for z in range(4):
                out[z, rows, :] = term[:, z * TOK : (z + 1) * TOK]


def norm_kernel(info, parts, hidden, gain, router, ids, residual_out, own_out, send_out, share_out, halves):
    core = info[1]
    square = jnp.zeros((1, TOK), f32)
    for lo in range(0, D, PART):
        rows = slice(lo, lo + PART)
        acc = hidden[rows, :].astype(f32)
        for z in range(4):
            acc = acc + parts[z, rows, :].astype(f32)
        rounded = acc.astype(bf16)
        residual_out[rows, :] = rounded
        res = rounded.astype(f32)
        square = square + jnp.sum(res * res, axis=0, keepdims=True)
    factor = lax.rsqrt(square * (1.0 / D) + norm_eps)
    logits = jnp.zeros((EXPERTS, TOK), f32)
    for half in range(2):
        base = half * HALF
        res = residual_out[base : base + HALF, :].astype(f32)
        normed = (res * factor * gain[base : base + HALF, :].astype(f32)).astype(bf16)
        halves[half] = normed
    for half in range(2):
        base = half * HALF
        logits += jnp.dot(router[half], halves[half], preferred_element_type=f32)
    expert = lax.broadcasted_iota(jnp.int32, (EXPERTS, TOK), 0)
    named = expert == ids[0:1, :]
    for k in range(1, TOP):
        named = named | (expert == ids[k : k + 1, :])
    raised = jnp.where(named, jnp.exp(logits), 0.0)
    share_out[...] = raised / jnp.sum(raised, axis=0, keepdims=True)
    own_out[...] = halves[core]
    send_out[...] = halves[1 - core]


def slots_of(ids, offset):
    expert = lax.broadcasted_iota(jnp.int32, (EXPERTS, TOK), 0)
    named = expert == ids[0:1, :]
    for k in range(1, TOP):
        named = named | (expert == ids[k : k + 1, :])
    before = lax.broadcasted_iota(jnp.int32, (TOK, TOK), 0) < lax.broadcasted_iota(
        jnp.int32, (TOK, TOK), 1
    )
    rank = jnp.dot(
        named.astype(f32).astype(bf16), before.astype(f32).astype(bf16), preferred_element_type=f32
    )
    row = rank + SLOTS * jnp.floor(rank * (1.0 / SLOTS)) + offset
    return jnp.where(named, row, -1.0)


def slot_rows(core, own_ids, other_ids):
    start = (core * SLOTS).astype(f32)
    return slots_of(own_ids, start), slots_of(other_ids, SLOTS - start)


def widened(rows):
    return jnp.concatenate([rows, jnp.zeros((rows.shape[0], WIDE - HALF), rows.dtype)], axis=1)


def dispatch_kernel(info, own, other, own_ids, other_ids, *refs):
    outs, slots = refs[:CHUNKS], refs[CHUNKS]
    slots[:, 0:TOK], slots[:, TOK : 2 * TOK] = slot_rows(info[1], own_ids, other_ids)
    tokens = jnp.concatenate([own[...], other[...]], axis=1)
    place = lax.broadcasted_iota(jnp.int32, (EXPERTS, PAIR_SLOTS, 2 * TOK), 1).astype(f32)
    for chunk in range(CHUNKS):
        hit = slots[...][:, None, :] == place + float(chunk * PAIR_SLOTS)
        pick = jnp.where(hit, 1.0, 0.0).reshape(ROWS, 2 * TOK).astype(bf16)
        rows = lax.dot_general(pick, tokens, NT, preferred_element_type=f32).astype(bf16)
        outs[chunk][...] = widened(rows)


def mixing_kernel(info, own_ids, other_ids, own_share, other_share, *outs):
    own_slot, other_slot = slot_rows(info[1], own_ids, other_ids)
    slot = jnp.concatenate([own_slot, other_slot], axis=1).T.astype(bf16)
    share = jnp.concatenate([own_share[...], other_share[...]], axis=1).T
    high = share.astype(bf16)
    rest = (share - high.astype(f32)).astype(bf16)
    expert = lax.broadcasted_iota(jnp.int32, (EXPERTS, ROWS), 0)
    column = lax.broadcasted_iota(jnp.int32, (EXPERTS, ROWS), 1)
    spread = jnp.where(column // PAIR_SLOTS == expert, 1.0, 0.0).astype(bf16)
    slot = jnp.dot(slot, spread, preferred_element_type=f32)
    high = jnp.dot(high, spread, preferred_element_type=f32)
    rest = jnp.dot(rest, spread, preferred_element_type=f32)
    place = (lax.broadcasted_iota(jnp.int32, (2 * TOK, ROWS), 1) % PAIR_SLOTS).astype(f32)
    for chunk in range(CHUNKS):
        hit = slot == place + float(chunk * PAIR_SLOTS)
        outs[chunk][0 : 2 * TOK, :] = jnp.where(hit, high, 0.0).astype(bf16)
        outs[chunk][2 * TOK : 4 * TOK, :] = jnp.where(hit, rest, 0.0).astype(bf16)


def expert_kernel(info, own, other, gate_w, up_w, down_w, keep_out, send_out):
    core = info[1]
    own_rows = pl.ds(pl.multiple_of(core * HALF, 32), HALF)
    other_rows = pl.ds(pl.multiple_of((1 - core) * HALF, 32), HALF)
    x_own = own[:, :HALF]
    x_other = other[:, :HALF]
    gate = jnp.dot(x_own, gate_w[own_rows, :], preferred_element_type=f32)
    gate += jnp.dot(x_other, gate_w[other_rows, :], preferred_element_type=f32)
    up = jnp.dot(x_own, up_w[own_rows, :], preferred_element_type=f32)
    up += jnp.dot(x_other, up_w[other_rows, :], preferred_element_type=f32)
    active = (gate * jax.nn.sigmoid(swiglu_alpha * gate) * (up + 1.0)).astype(bf16)
    for rows, ref in ((other_rows, send_out), (own_rows, keep_out)):
        piece = lax.dot_general(active, down_w[rows, :], NT, preferred_element_type=f32)
        ref[...] = widened(piece.astype(bf16))


def mixed(factors, rows):
    both = jnp.dot(factors[...], rows[:, :HALF], preferred_element_type=f32)
    return both[: 2 * TOK] + both[2 * TOK :]


def first_mix_kernel(factors, rows, out):
    out[...] = mixed(factors, rows)


def next_mix_kernel(factors, rows, so_far, out):
    out[...] = so_far[...] + mixed(factors, rows)


def last_mix_kernel(factors, rows, so_far, own_out, send_out):
    total = so_far[...] + mixed(factors, rows)
    for lo in range(0, HALF, TOK):
        hi = min(lo + TOK, HALF)
        own_out[lo:hi, :] = total[:TOK, lo:hi].T
        send_out[lo:hi, :] = total[TOK:, lo:hi].T


def final_kernel(info, residual, own, other, out):
    core = info[1]
    for half, ref in ((core, own), (1 - core, other)):
        for lo in range(0, HALF, PART):
            rows = pl.ds(pl.multiple_of(half * HALF + lo, 32), PART)
            mix = ref[lo : lo + PART, :]
            out[rows, :] = (residual[rows, :].astype(f32) + mix).astype(bf16)


def params(mib):
    return pltpu.CompilerParams(vmem_limit_bytes=mib << 20)


def kernel_call(body, outs, operands, with_info=True, scratch=(), mib=40, flops=0, moved=0):
    single = not isinstance(outs, list)
    specs = [SMEM_SPEC] * int(with_info) + [VMEM_SPEC] * (len(operands) - int(with_info))
    return pl.pallas_call(
        body,
        out_shape=outs,
        in_specs=specs,
        out_specs=VMEM_SPEC if single else [VMEM_SPEC] * len(outs),
        scratch_shapes=list(scratch),
        compiler_params=params(mib),
        cost_estimate=pl.CostEstimate(flops=flops, bytes_accessed=moved, transcendentals=0),
    )(*operands)


def shape(*dims, dtype=bf16):
    return jax.ShapeDtypeStruct(dims, dtype)


def local(
    hidden_in,
    queries,
    key_heads,
    values,
    doc_lengths,
    out_weight,
    norm_gain,
    router_weight,
    expert_ids,
    gate_weight,
    up_weight,
    down_weight,
):
    upper = lax.axis_index("xh")
    core = lax.axis_index("c")
    info = jnp.stack([upper, core, doc_lengths[0]]).astype(jnp.int32)
    swap = [(0, 1), (1, 0)]

    lower_keys = lax.ppermute(key_heads[0], "xh", [(0, 1)])
    lower_values = lax.ppermute(values[0], "xh", [(0, 1)])
    prepared = kernel_call(
        prepare_kernel,
        shape(4, TOK, 1536),
        (queries[0], key_heads[0], values[0], lower_keys, lower_values),
        with_info=False,
    )
    qkv = lax.all_to_all(prepared, "z", split_axis=0, concat_axis=0, tiled=True).reshape(512, 1536)

    own_w = out_weight.T
    half_w = lax.dynamic_slice_in_dim(own_w, core * HALF, HALF, axis=0)
    first_w = lax.ppermute(half_w, ("xh", "xl"), [(0, 3), (3, 0), (1, 2), (2, 1)])
    first_w, qkv = lax.optimization_barrier((first_w, qkv))
    second_w = lax.ppermute(first_w, "c", swap)

    ids = expert_ids[0].T
    other_ids = lax.ppermute(ids, "c", swap)

    att = kernel_call(
        attention_kernel,
        shape(512, 1024),
        (info, qkv),
        scratch=(pltpu.VMEM((4, 1024, 128), bf16), pltpu.VMEM((4, 1024, 256), bf16)),
        flops=8 * 10**9,
    )
    partial = kernel_call(
        project_kernel,
        shape(4, D, TOK),
        (info, att, own_w, first_w, second_w),
        flops=3 * 10**9,
    )
    parts = lax.all_to_all(partial, "z", split_axis=0, concat_axis=0, tiled=True)

    gain = jnp.broadcast_to(norm_gain[:, None], (D, TOK))
    router = router_weight.T.reshape(EXPERTS, 2, HALF).transpose(1, 0, 2)
    residual, own_half, send_half, share = kernel_call(
        norm_kernel,
        [shape(D, TOK), shape(HALF, TOK), shape(HALF, TOK), shape(EXPERTS, TOK, dtype=f32)],
        (info, parts, hidden_in[0].T, gain, router, ids),
        scratch=(pltpu.VMEM((2, HALF, TOK), bf16),),
    )
    other_half = lax.ppermute(send_half, "c", swap)
    other_share = lax.ppermute(share, "c", swap)

    outgoing = kernel_call(
        dispatch_kernel,
        [shape(ROWS, WIDE)] * CHUNKS,
        (info, own_half, other_half, ids, other_ids),
        scratch=(pltpu.VMEM((EXPERTS, 2 * TOK), f32),),
    )
    factors = kernel_call(
        mixing_kernel,
        [shape(4 * TOK, ROWS)] * CHUNKS,
        (info, ids, other_ids, share, other_share),
    )
    chips = ("xh", "z", "xl", "y")
    down_w = down_weight[0].T

    def across(rows):
        return lax.all_to_all(
            rows.reshape(EXPERTS, PAIR_SLOTS, WIDE), chips, split_axis=0, concat_axis=0, tiled=True
        ).reshape(ROWS, WIDE)

    summed = []
    for chunk in range(CHUNKS):
        arrived = across(outgoing[chunk])
        arrived_other = lax.ppermute(arrived, "c", swap)
        keep, send = kernel_call(
            expert_kernel,
            [shape(ROWS, WIDE)] * 2,
            (info, arrived, arrived_other, gate_weight[0], up_weight[0], down_w),
            mib=56,
            flops=7 * 10**9,
            moved=16 * 10**6,
        )
        sent = lax.ppermute(send, "c", swap)
        summed.append((keep.astype(f32) + sent.astype(f32)).astype(bf16))

    mix = kernel_call(
        first_mix_kernel, shape(2 * TOK, HALF, dtype=f32), (factors[0], across(summed[0])), with_info=False
    )
    mix = kernel_call(
        next_mix_kernel, shape(2 * TOK, HALF, dtype=f32), (factors[1], across(summed[1]), mix), with_info=False
    )
    own_mix, send_mix = kernel_call(
        last_mix_kernel, [shape(HALF, TOK, dtype=f32)] * 2, (factors[2], across(summed[2]), mix), with_info=False
    )
    other_mix = lax.ppermute(send_mix, "c", swap)
    layer_out = kernel_call(final_kernel, shape(D, TOK), (info, residual, own_mix, other_mix))
    return layer_out.T[None]


def solution(mesh):
    split_mesh = Mesh(mesh.devices.reshape(2, 4, 2, 4, 2), ("xh", "z", "xl", "y", "c"))
    seq = ("xh", "z")
    doc = ("xl", "y", "c")
    in_specs = (
        P(doc, seq, None),
        P(doc, seq, None),
        P(doc, seq, None),
        P(doc, seq, None),
        P(doc),
        P(seq, None),
        P(),
        P(),
        P(doc, seq, None),
        P(seq + doc, None, None),
        P(seq + doc, None, None),
        P(seq + doc, None, None),
    )
    return jax.shard_map(
        local,
        mesh=split_mesh,
        in_specs=in_specs,
        out_specs=P(doc, seq, None),
        check_vma=False,
    )
```

```python
import functools
import jax
import jax.numpy as jnp
from jax import lax
from jax.experimental import pallas as pl
from jax.experimental.pallas import tpu as pltpu
from jax.sharding import Mesh, PartitionSpec as P

HD = 64
TOP = 4
EXPERTS = 64
TOK = 128
D = 2880
FF = 768
HALF = D // 2
WIDE = 1536
CAP = 12
PAIR_ROWS = 2 * CAP
ROWS = EXPERTS * PAIR_ROWS
PART = 480
STEPS = ((0, 256), (256, 640), (896, 640))

negative_fill = -1e30
swiglu_alpha = 1.702
norm_eps = 1e-05
exp_scale = HD ** (-0.5) * 1.4426950408889634

f32 = jnp.float32
bf16 = jnp.bfloat16
VMEM_SPEC = pl.BlockSpec(memory_space=pltpu.VMEM)
SMEM_SPEC = pl.BlockSpec(memory_space=pltpu.SMEM)
ANY_SPEC = pl.BlockSpec(memory_space=pl.ANY)
DMA = pltpu.SemaphoreType.DMA
NT = (((1,), (1,)), ((), ()))


def prepare_kernel(queries, key_heads, values, lower_keys, lower_values, out):
    lane = lax.broadcasted_iota(jnp.int32, (TOK, 128), 1)
    for z in range(4):
        out[z, :, 0:512] = queries[:, z * 512 : z * 512 + 512]
        out[z, :, 512:1024] = queries[:, 2048 + z * 512 : 2560 + z * 512]
        tile = (z // 2) * 128
        for n, ref in enumerate((key_heads, values, lower_keys, lower_values)):
            first = ref[:, tile : tile + 128].astype(f32)
            second = ref[:, 256 + tile : 384 + tile].astype(f32)
            if z % 2 == 0:
                second = pltpu.roll(second, 64, 1)
            else:
                first = pltpu.roll(first, 64, 1)
            out[z, :, 1024 + 128 * n : 1152 + 128 * n] = jnp.where(
                lane < 64, first, second
            ).astype(bf16)


def attention_kernel(a, info, qkv, att, keys, vals):
    upper = info[0]
    doc_len = info[2]
    lane = lax.broadcasted_iota(jnp.int32, (512, 128), 1)
    low = lane < 64
    one = jnp.ones((512, 128), f32)
    for side in range(2):
        base = 1280 - 256 * side
        rows = pl.ds(512 * side, 512)
        kk = qkv[:, base : base + 128].astype(f32)
        vv = qkv[:, base + 128 : base + 256].astype(f32)
        kr = pltpu.roll(kk, 64, 1)
        vr = pltpu.roll(vv, 64, 1)
        for par in range(2):
            keep = low if par == 0 else ~low
            keys[par, rows, :] = jnp.where(keep, kk if a == par else kr, 0.0).astype(bf16)
            vals[par, rows, 0:128] = jnp.where(keep, vv if a == par else vr, 0.0).astype(bf16)
            vals[par, rows, 128:256] = jnp.where(keep, one, 0.0).astype(bf16)

    row_id = lax.broadcasted_iota(jnp.int32, (128, 128), 0)
    col_id = lax.broadcasted_iota(jnp.int32, (128, 128), 1)

    def block(pair, i, with_other):
        nk = (i + 1) * 128 + (512 if with_other else 0)
        start = 0 if with_other else 512
        q_rows = slice(i * 128, (i + 1) * 128)
        q_base = pl.multiple_of(pair * 256, 256)
        q_tiles = [
            qkv[q_rows, pl.ds(pl.multiple_of(a * 512 + q_base + 128 * t, 128), 128)]
            for t in range(2)
        ]
        q_stack = jnp.concatenate(q_tiles, axis=0)
        position = lax.broadcasted_iota(jnp.int32, (1, nk), 1)
        length_bias = jnp.where(position < doc_len, 0.0, negative_fill)
        query = row_id + (nk - 128)
        diag = jnp.where(col_id <= row_id, 0.0, negative_fill) + length_bias[:, nk - 128 :]
        diag = jnp.concatenate([diag] * 2, axis=0)
        total = None
        for par in range(2):
            k_blk = keys[par, start : start + nk, :]
            scores = lax.dot_general(q_stack, k_blk, NT, preferred_element_type=f32)
            last = scores[:, nk - 128 :] + diag
            if nk > 128:
                scores = jnp.concatenate(
                    [scores[:, : nk - 128] + length_bias[:, : nk - 128], last], axis=1
                )
            else:
                scores = last
            top = jnp.max(scores, axis=1, keepdims=True)
            weights = jnp.exp2((scores - top) * exp_scale).astype(bf16)
            part = jnp.dot(
                weights, vals[par, start : start + nk, :], preferred_element_type=f32
            )
            total = part if total is None else total + part
        result = (total[:, 0:128] / total[:, 128:256]).astype(bf16)
        for t in range(2):
            att[q_rows, pl.ds(pl.multiple_of(q_base + 128 * t, 128), 128)] = result[
                128 * t : 128 * (t + 1)
            ]

    def all_blocks(with_other):
        def body(n, carry):
            for i in range(4):
                block(n, i, with_other)
            return carry

        lax.fori_loop(0, 2, body, 0)

    pl.when(upper == 1)(lambda: all_blocks(True))
    pl.when(upper == 0)(lambda: all_blocks(False))


def pick_attended(upper, first_att, second_att, rows):
    first, second = first_att[rows, :], second_att[rows, :]
    return jnp.where(upper == 0, first, second), jnp.where(upper == 0, second, first)


def project(core, own, other, own_w, first_w, second_w, store):
    for half in range(2):
        for lo in range(0, HALF, PART):
            rows = slice(half * HALF + lo, half * HALF + lo + PART)
            far = slice(lo, lo + PART)
            far_w = jnp.where(core == half, first_w[far, :], second_w[far, :])
            term = lax.dot_general(own_w[rows, :], own, NT, preferred_element_type=f32)
            term += lax.dot_general(far_w, other, NT, preferred_element_type=f32)
            store(half, far, term)


def token_block(z, shift):
    return pl.ds(pl.multiple_of(lax.rem(z + shift, 4) * TOK, TOK), TOK)


def far_kernel(info, first_att, second_att, own_w, first_w, second_w, low_out, high_out):
    own, other = pick_attended(info[0], first_att, second_att, token_block(info[3], 2))

    def store(half, rows, term):
        (low_out, high_out)[half][rows, :] = term.astype(bf16)

    project(info[1], own, other, own_w, first_w, second_w, store)


def near_kernel(
    info, first_att, second_att, own_w, first_w, second_w, up_low, up_high, down_low, down_high, own_out
):
    picked = [
        pick_attended(info[0], first_att, second_att, token_block(info[3], shift))
        for shift in (1, 3, 0)
    ]
    own = jnp.concatenate([p[0] for p in picked], axis=0)
    other = jnp.concatenate([p[1] for p in picked], axis=0)

    def store(half, rows, term):
        up, down = ((up_low, down_low), (up_high, down_high))[half]
        up[rows, :] = term[:, :TOK].astype(up.dtype)
        down[rows, :] = term[:, TOK : 2 * TOK].astype(down.dtype)
        own_out[slice(half * HALF + rows.start, half * HALF + rows.stop), :] = term[:, 2 * TOK :]

    project(info[1], own, other, own_w, first_w, second_w, store)


def stage_kernel(info, gate_w, up_w, down_w, ready, gate_out, up_out, down_out, sems):
    own_rows = pl.ds(pl.multiple_of(info[1] * HALF, 32), HALF)
    copies = [
        pltpu.make_async_copy(gate_w, gate_out, sems.at[0]),
        pltpu.make_async_copy(up_w, up_out, sems.at[1]),
        pltpu.make_async_copy(down_w.at[own_rows, :], down_out, sems.at[2]),
    ]
    for copy in copies:
        copy.start()
    for copy in copies:
        copy.wait()


def norm_kernel(
    info,
    own_part,
    low_a,
    low_b,
    high_a,
    high_b,
    hidden,
    gain,
    router,
    ids,
    residual_out,
    own_out,
    send_out,
    share_out,
    normed,
    held,
    sems,
):
    core = info[1]
    copies = [
        pltpu.make_async_copy(ref, held.at[n], sems.at[n])
        for n, ref in enumerate((low_a, low_b, high_a, high_b))
    ]
    for copy in copies:
        copy.start()
    for copy in copies:
        copy.wait()
    square = jnp.zeros((1, TOK), f32)
    for half in range(2):
        for lo in range(0, HALF, PART):
            rows = slice(half * HALF + lo, half * HALF + lo + PART)
            acc = hidden[rows, :].astype(f32) + own_part[rows, :]
            acc = acc + held[2 * half, lo : lo + PART, :].astype(f32)
            acc = acc + held[2 * half + 1, lo : lo + PART, :].astype(f32)
            rounded = acc.astype(bf16)
            residual_out[rows, :] = rounded
            res = rounded.astype(f32)
            square = square + jnp.sum(res * res, axis=0, keepdims=True)
    factor = lax.rsqrt(square * (1.0 / D) + norm_eps)
    for lo in range(0, D, PART):
        rows = slice(lo, lo + PART)
        res = residual_out[rows, :].astype(f32)
        normed[rows, :] = (res * factor * gain[rows, :].astype(f32)).astype(bf16)
    logits = jnp.dot(router[...], normed[...], preferred_element_type=f32)
    named = named_of(ids[...])
    raised = jnp.where(named, jnp.exp(logits), 0.0)
    share_out[...] = raised / jnp.sum(raised, axis=0, keepdims=True)
    own_out[...] = normed[pl.ds(pl.multiple_of(core * HALF, 32), HALF), :]
    send_out[:HALF, :] = normed[pl.ds(pl.multiple_of((1 - core) * HALF, 32), HALF), :]
    send_out[HALF:, :] = jnp.concatenate(
        [ids[...].astype(f32), jnp.zeros((16 - TOP, TOK), f32)], axis=0
    ).astype(bf16)


def named_of(ids):
    expert = lax.broadcasted_iota(jnp.int32, (EXPERTS, TOK), 0)
    named = expert == ids[0:1, :]
    for k in range(1, TOP):
        named = named | (expert == ids[k : k + 1, :])
    return named


def slots_of(ids, offset):
    named = named_of(ids)
    before = lax.broadcasted_iota(jnp.int32, (TOK, TOK), 0) < lax.broadcasted_iota(
        jnp.int32, (TOK, TOK), 1
    )
    rank = jnp.dot(
        named.astype(f32).astype(bf16), before.astype(f32).astype(bf16), preferred_element_type=f32
    )
    return jnp.where(named, rank + offset, -1.0)


def slot_rows(core, own_ids, other):
    start = (core * CAP).astype(f32)
    other_ids = other[HALF:, :].astype(f32).astype(jnp.int32)
    return slots_of(own_ids[...], start), slots_of(other_ids, CAP - start)


def widened(rows):
    return jnp.concatenate([rows, jnp.zeros((rows.shape[0], WIDE - HALF), rows.dtype)], axis=1)


EXPERT_BLOCK = 16
ROW_BLOCK = EXPERT_BLOCK * PAIR_ROWS


def dispatch_kernel(info, own, other, own_ids, out, slots):
    slots[:, 0:TOK], slots[:, TOK : 2 * TOK] = slot_rows(info[1], own_ids, other)
    tokens = jnp.concatenate([own[...], other[:HALF, :]], axis=1)
    place = lax.broadcasted_iota(jnp.int32, (EXPERT_BLOCK, PAIR_ROWS, 2 * TOK), 1).astype(f32)
    for n in range(EXPERTS // EXPERT_BLOCK):
        block = slots[n * EXPERT_BLOCK : (n + 1) * EXPERT_BLOCK, :]
        hit = block[:, None, :] == place
        pick = jnp.where(hit, 1.0, 0.0).reshape(ROW_BLOCK, 2 * TOK).astype(bf16)
        rows = lax.dot_general(pick, tokens, NT, preferred_element_type=f32).astype(bf16)
        out[n * ROW_BLOCK : (n + 1) * ROW_BLOCK, :] = widened(rows)


def mixing_kernel(info, own_ids, other, own_share, other_share, out):
    own_slot, other_slot = slot_rows(info[1], own_ids, other)
    slot = jnp.concatenate([own_slot, other_slot], axis=1).T.astype(bf16)
    share = jnp.concatenate([own_share[...], other_share[...]], axis=1).T
    high = share.astype(bf16)
    rest = (share - high.astype(f32)).astype(bf16)
    expert = lax.broadcasted_iota(jnp.int32, (EXPERTS, ROWS), 0) * PAIR_ROWS
    offset = lax.broadcasted_iota(jnp.int32, (EXPERTS, ROWS), 1) - expert
    inside = (offset >= 0) & (offset < PAIR_ROWS)
    spread = jnp.where(inside, 1.0, 0.0).astype(bf16)
    place = jnp.sum(jnp.where(inside, offset.astype(f32), 0.0), axis=0, keepdims=True)
    hit = jnp.dot(slot, spread, preferred_element_type=f32) == place
    for part, factor in enumerate((high, rest)):
        wide = jnp.dot(factor, spread, preferred_element_type=f32)
        out[part * 2 * TOK : (part + 1) * 2 * TOK, :] = jnp.where(hit, wide, 0.0).astype(bf16)


def active_kernel(info, own, other, gate_w, up_w, out):
    core = info[1]
    own_rows = pl.ds(pl.multiple_of(core * HALF, 32), HALF)
    other_rows = pl.ds(pl.multiple_of((1 - core) * HALF, 32), HALF)
    x_own = own[:, :HALF]
    x_other = other[:, :HALF]
    gate = jnp.dot(x_own, gate_w[own_rows, :], preferred_element_type=f32)
    gate += jnp.dot(x_other, gate_w[other_rows, :], preferred_element_type=f32)
    up = jnp.dot(x_own, up_w[own_rows, :], preferred_element_type=f32)
    up += jnp.dot(x_other, up_w[other_rows, :], preferred_element_type=f32)
    out[...] = (gate * jax.nn.sigmoid(swiglu_alpha * gate) * (up + 1.0)).astype(bf16)


def down_kernel(starts, info, *refs):
    count = len(starts)
    own, other = refs[:count], refs[count : 2 * count]
    down_w, other_w = refs[2 * count : 2 * count + 2]
    out, held, sems = refs[-3:]
    copies = []
    for n, start in enumerate(starts):
        rows = own[n].shape[0]
        first = lax.dot_general(own[n][...], down_w[...], NT, preferred_element_type=f32)
        second = lax.dot_general(other[n][...], other_w[...], NT, preferred_element_type=f32)
        both = first.astype(bf16).astype(f32) + second.astype(bf16).astype(f32)
        held[n, :rows, :] = widened(both.astype(bf16))
        copy = pltpu.make_async_copy(
            held.at[n, pl.ds(0, rows)], out.at[pl.ds(start, rows)], sems.at[n]
        )
        copy.start()
        copies.append(copy)
    for copy in copies:
        copy.wait()


MIX_BLOCK = 512


def mix_kernel(factors, rows, own_out, send_out):
    both = jnp.dot(factors[...], rows[...], preferred_element_type=f32)
    total = both[: 2 * TOK] + both[2 * TOK :]
    own_out[...] = total[:TOK].T
    send_out[...] = total[TOK:].T


def final_kernel(info, residual, own, other, out):
    core = info[1]
    for half, ref in ((core, own), (1 - core, other)):
        for lo in range(0, HALF, PART):
            rows = pl.ds(pl.multiple_of(half * HALF + lo, 32), PART)
            mix = ref[lo : lo + PART, :]
            out[rows, :] = (residual[rows, :].astype(f32) + mix).astype(bf16)


def params(mib):
    return pltpu.CompilerParams(vmem_limit_bytes=mib << 20)


def kernel_call(body, outs, operands, with_info=True, scratch=(), mib=40, flops=0, moved=0, remain=()):
    single = not isinstance(outs, list)
    specs = [SMEM_SPEC] * int(with_info) + [VMEM_SPEC] * (len(operands) - int(with_info))
    for n in remain:
        specs[n] = ANY_SPEC
    return pl.pallas_call(
        body,
        out_shape=outs,
        in_specs=specs,
        out_specs=VMEM_SPEC if single else [VMEM_SPEC] * len(outs),
        scratch_shapes=list(scratch),
        compiler_params=params(mib),
        cost_estimate=pl.CostEstimate(flops=flops, bytes_accessed=moved, transcendentals=0),
    )(*operands)


def shape(*dims, dtype=bf16):
    return jax.ShapeDtypeStruct(dims, dtype)


def local(
    hidden_in,
    queries,
    key_heads,
    values,
    doc_lengths,
    out_weight,
    norm_gain,
    router_weight,
    expert_ids,
    gate_weight,
    up_weight,
    down_weight,
):
    upper = lax.axis_index("xh")
    core = lax.axis_index("c")
    depth = lax.axis_index("z")
    info = jnp.stack([upper, core, doc_lengths[0], depth]).astype(jnp.int32)
    swap = [(0, 1), (1, 0)]

    lower_keys = lax.ppermute(key_heads[0], "xh", [(0, 1)])
    lower_values = lax.ppermute(values[0], "xh", [(0, 1)])
    prepared = kernel_call(
        prepare_kernel,
        shape(4, TOK, 1536),
        (queries[0], key_heads[0], values[0], lower_keys, lower_values),
        with_info=False,
    )
    qkv = lax.all_to_all(prepared, "z", split_axis=0, concat_axis=0, tiled=True).reshape(512, 1536)

    own_w = out_weight.T
    half_w = lax.dynamic_slice_in_dim(own_w, core * HALF, HALF, axis=0)
    first_w = lax.ppermute(half_w, ("xh", "xl"), [(0, 3), (3, 0), (1, 2), (2, 1)])

    ids = expert_ids[0].T

    def attend(a, qkv):
        return kernel_call(
            functools.partial(attention_kernel, a),
            shape(512, 512),
            (info, qkv),
            scratch=(pltpu.VMEM((2, 1024, 128), bf16), pltpu.VMEM((2, 1024, 256), bf16)),
            flops=4 * 10**9,
            mib=16,
        )

    first_w, qkv = lax.optimization_barrier((first_w, qkv))
    second_w = lax.ppermute(first_w, "c", swap)
    first_att = attend(0, qkv)
    second_att = attend(1, qkv)

    plus = [(i, (i + 1) % 4) for i in range(4)]
    minus = [(i, (i + 3) % 4) for i in range(4)]
    weights = (own_w, first_w, second_w)
    half_shape = shape(HALF, TOK)
    half_float = shape(HALF, TOK, dtype=f32)
    far_low, far_high = kernel_call(
        far_kernel,
        [half_shape] * 2,
        (info, first_att, second_att) + weights,
        flops=10**9,
        mib=12,
    )
    far_low = lax.ppermute(far_low, "z", plus)
    far_high = lax.ppermute(far_high, "z", minus)
    up_low, up_high, down_low, down_high, own_part = kernel_call(
        near_kernel,
        [half_float, half_shape, half_shape, half_float, shape(D, TOK, dtype=f32)],
        (info, first_att, second_att) + weights,
        flops=3 * 10**9,
        mib=16,
    )
    high_a = lax.ppermute(up_high, "z", plus)
    low_b = lax.ppermute(down_low, "z", minus)
    low_a = lax.ppermute((up_low + far_low.astype(f32)).astype(bf16), "z", plus)
    high_b = lax.ppermute((down_high + far_high.astype(f32)).astype(bf16), "z", minus)

    down_w = down_weight[0].T
    other_down = lax.ppermute(
        lax.dynamic_slice_in_dim(down_w, (1 - core) * HALF, HALF, axis=0), "c", swap
    )
    gate_v, up_v, down_v = pl.pallas_call(
        stage_kernel,
        out_shape=[pltpu.VMEM((D, FF), bf16)] * 2 + [pltpu.VMEM((HALF, FF), bf16)],
        in_specs=[SMEM_SPEC] + [ANY_SPEC] * 4,
        out_specs=[VMEM_SPEC] * 3,
        scratch_shapes=[DMA((3,))],
        compiler_params=params(16),
    )(info, gate_weight[0], up_weight[0], down_w, down_low)
    gain = jnp.broadcast_to(norm_gain[:, None], (D, TOK))
    gain, other_down, gate_v, up_v, down_v = lax.optimization_barrier(
        (gain, other_down, gate_v, up_v, down_v)
    )
    residual, own_half, send_half, share = kernel_call(
        norm_kernel,
        [shape(D, TOK), half_shape, shape(HALF + 16, TOK), shape(EXPERTS, TOK, dtype=f32)],
        (info, own_part, low_a, low_b, high_a, high_b, hidden_in[0].T, gain, router_weight.T, ids),
        scratch=(pltpu.VMEM((D, TOK), bf16), pltpu.VMEM((4, HALF, TOK), bf16), DMA((4,))),
        remain=(2, 3, 4, 5),
        mib=12,
    )
    other_half = lax.ppermute(send_half, "c", swap)
    other_share = lax.ppermute(share, "c", swap)

    outgoing = kernel_call(
        dispatch_kernel,
        shape(ROWS, WIDE),
        (info, own_half, other_half, ids),
        scratch=(pltpu.VMEM((EXPERTS, 2 * TOK), f32),),
        mib=16,
    )
    factors = kernel_call(
        mixing_kernel,
        shape(4 * TOK, ROWS),
        (info, ids, other_half, share, other_share),
        mib=16,
    )
    chips = ("xh", "z", "xl", "y")

    def across(rows):
        return lax.all_to_all(
            rows.reshape(EXPERTS, PAIR_ROWS, WIDE), chips, split_axis=0, concat_axis=0, tiled=True
        ).reshape(ROWS, WIDE)

    arrived = across(outgoing)
    own_active, other_active = [], []
    for start, count in STEPS:
        rows = arrived[start : start + count]
        if own_active:
            rows, rows_other = lax.optimization_barrier((rows, rows_other))
        rows_other = lax.ppermute(rows, "c", swap)
        active = kernel_call(
            active_kernel,
            shape(count, FF),
            (info, rows, rows_other, gate_v, up_v),
            flops=45 * 10**8,
            mib=20,
        )
        own_active.append(active)
        other_active.append(lax.ppermute(active, "c", swap))

    def down(steps, *buffer):
        picked = [own_active[n] for n in steps] + [other_active[n] for n in steps]
        rows = max(STEPS[n][1] for n in steps)
        operands = (info, *picked, down_v, other_down, *buffer)
        return pl.pallas_call(
            functools.partial(down_kernel, [STEPS[n][0] for n in steps]),
            out_shape=pltpu.HBM((ROWS, WIDE), bf16),
            in_specs=[SMEM_SPEC] + [VMEM_SPEC] * (len(picked) + 2) + [ANY_SPEC] * len(buffer),
            out_specs=pl.BlockSpec(memory_space=pltpu.HBM),
            scratch_shapes=[pltpu.VMEM((len(steps), rows, WIDE), bf16), DMA((len(steps),))],
            input_output_aliases={len(operands) - 1: 0} if buffer else {},
            compiler_params=params(24),
        )(*operands)

    expert_out = down([2], down([0, 1]))
    own_mix, send_mix = pl.pallas_call(
        mix_kernel,
        grid=(WIDE // MIX_BLOCK,),
        out_shape=[shape(WIDE, TOK, dtype=f32)] * 2,
        in_specs=[
            pl.BlockSpec((4 * TOK, ROWS), lambda i: (0, 0)),
            pl.BlockSpec((ROWS, MIX_BLOCK), lambda i: (0, i)),
        ],
        out_specs=[pl.BlockSpec((MIX_BLOCK, TOK), lambda i: (i, 0))] * 2,
        compiler_params=params(32),
    )(factors, across(expert_out))
    other_mix = lax.ppermute(send_mix, "c", swap)
    layer_out = kernel_call(
        final_kernel, shape(D, TOK), (info, residual, own_mix, other_mix), mib=12
    )
    return layer_out.T[None]


def solution(mesh):
    split_mesh = Mesh(mesh.devices.reshape(2, 4, 2, 4, 2), ("xh", "z", "xl", "y", "c"))
    seq = ("xh", "z")
    doc = ("xl", "y", "c")
    in_specs = (
        P(doc, seq, None),
        P(doc, seq, None),
        P(doc, seq, None),
        P(doc, seq, None),
        P(doc),
        P(seq, None),
        P(),
        P(),
        P(doc, seq, None),
        P(seq + doc, None, None),
        P(seq + doc, None, None),
        P(seq + doc, None, None),
    )
    return jax.shard_map(
        local,
        mesh=split_mesh,
        in_specs=in_specs,
        out_specs=P(doc, seq, None),
        check_vma=False,
    )
```

```python
import functools
import jax
import jax.numpy as jnp
from jax import lax
from jax.experimental import pallas as pl
from jax.experimental.pallas import tpu as pltpu
from jax.sharding import Mesh, PartitionSpec as P

HD = 64
TOP = 4
EXPERTS = 64
TOK = 128
D = 2880
FF = 768
HALF = D // 2
WIDE = 1536
CAP = 12
PAIR_ROWS = 2 * CAP
ROWS = EXPERTS * PAIR_ROWS
PART = 480
STEPS = ((0, 256), (256, 640), (896, 640))

negative_fill = -1e30
swiglu_alpha = 1.702
norm_eps = 1e-05
exp_scale = HD ** (-0.5) * 1.4426950408889634

f32 = jnp.float32
bf16 = jnp.bfloat16
VMEM_SPEC = pl.BlockSpec(memory_space=pltpu.VMEM)
SMEM_SPEC = pl.BlockSpec(memory_space=pltpu.SMEM)
HBM_SPEC = pl.BlockSpec(memory_space=pltpu.HBM)
ANY_SPEC = pl.BlockSpec(memory_space=pl.ANY)
DMA = pltpu.SemaphoreType.DMA
NT = (((1,), (1,)), ((), ()))


def prepare_kernel(queries, key_heads, values, out):
    lane = lax.broadcasted_iota(jnp.int32, (TOK, 128), 1)
    for z in range(4):
        out[z, :, 0:512] = queries[:, z * 512 : z * 512 + 512]
        out[z, :, 512:1024] = queries[:, 2048 + z * 512 : 2560 + z * 512]
        tile = (z // 2) * 128
        for n, ref in enumerate((key_heads, values)):
            first = ref[:, tile : tile + 128].astype(f32)
            second = ref[:, 256 + tile : 384 + tile].astype(f32)
            if z % 2 == 0:
                second = pltpu.roll(second, 64, 1)
            else:
                first = pltpu.roll(first, 64, 1)
            out[z, :, 1024 + 128 * n : 1152 + 128 * n] = jnp.where(
                lane < 64, first, second
            ).astype(bf16)


def attention_kernel(a, info, qkv, lower, att, keys, vals):
    upper = info[0]
    doc_len = info[2]
    lane = lax.broadcasted_iota(jnp.int32, (512, 128), 1)
    low = lane < 64
    one = jnp.ones((512, 128), f32)
    row = lax.broadcasted_iota(jnp.int32, (512, 128), 0)
    for side in range(2):
        rows = pl.ds(512 * side, 512)
        source = qkv[:, 1024:1280] if side else lower[...]
        kk = source[:, 0:128].astype(f32)
        vv = source[:, 128:256].astype(f32)
        kr = pltpu.roll(kk, 64, 1)
        vr = pltpu.roll(vv, 64, 1)
        position = row + 512 * upper if side else row
        masked = (lane == 0) & (position >= doc_len)
        bias = jnp.where(masked, negative_fill, 0.0).astype(bf16)
        for par in range(2):
            keep = low if par == 0 else ~low
            keys[par, rows, 0:128] = jnp.where(keep, kk if a == par else kr, 0.0).astype(bf16)
            keys[par, rows, 128:256] = bias
            vals[par, rows, 0:128] = jnp.where(keep, vv if a == par else vr, 0.0).astype(bf16)
            vals[par, rows, 128:256] = jnp.where(keep, one, 0.0).astype(bf16)

    first_lane = jnp.where(lane == 0, 1.0, 0.0).astype(bf16)
    causal = jnp.where(
        lax.broadcasted_iota(jnp.int32, (128, 128), 1)
        <= lax.broadcasted_iota(jnp.int32, (128, 128), 0),
        0.0,
        negative_fill,
    )
    causal = jnp.concatenate([causal] * 4, axis=0)

    def block(i, with_other):
        nk = (i + 1) * 128 + (512 if with_other else 0)
        start = 0 if with_other else 512
        q_rows = slice(i * 128, (i + 1) * 128)
        q_tiles = [qkv[q_rows, a * 512 + 128 * t : a * 512 + 128 * (t + 1)] for t in range(4)]
        q_stack = jnp.concatenate([jnp.concatenate(q_tiles, axis=0), first_lane], axis=1)
        total = None
        for par in range(2):
            k_blk = keys[par, start : start + nk, :]
            scores = lax.dot_general(q_stack, k_blk, NT, preferred_element_type=f32)
            last = scores[:, nk - 128 :] + causal
            if nk > 128:
                scores = jnp.concatenate([scores[:, : nk - 128], last], axis=1)
            else:
                scores = last
            top = jnp.max(scores, axis=1, keepdims=True)
            weights = jnp.exp2((scores - top) * exp_scale).astype(bf16)
            part = jnp.dot(
                weights, vals[par, start : start + nk, :], preferred_element_type=f32
            )
            total = part if total is None else total + part
        result = (total[:, 0:128] / total[:, 128:256]).astype(bf16)
        for t in range(4):
            att[q_rows, 128 * t : 128 * (t + 1)] = result[128 * t : 128 * (t + 1)]

    @pl.when(upper == 1)
    def _():
        for i in range(4):
            block(i, True)

    @pl.when(upper == 0)
    def _():
        for i in range(4):
            block(i, False)


def pick_attended(upper, first_att, second_att, rows):
    first, second = first_att[rows, :], second_att[rows, :]
    return jnp.where(upper == 0, first, second), jnp.where(upper == 0, second, first)


def project(core, own, other, own_w, first_w, second_w, store):
    for half in range(2):
        for lo in range(0, HALF, PART):
            rows = slice(half * HALF + lo, half * HALF + lo + PART)
            far = slice(lo, lo + PART)
            far_w = jnp.where(core == half, first_w[far, :], second_w[far, :])
            term = lax.dot_general(own_w[rows, :], own, NT, preferred_element_type=f32)
            term += lax.dot_general(far_w, other, NT, preferred_element_type=f32)
            store(half, far, term)


def token_block(z, shift):
    return pl.ds(pl.multiple_of(lax.rem(z + shift, 4) * TOK, TOK), TOK)


def far_kernel(info, first_att, second_att, own_w, first_w, second_w, low_out, high_out):
    own, other = pick_attended(info[0], first_att, second_att, token_block(info[3], 2))

    def store(half, rows, term):
        (low_out, high_out)[half][rows, :] = term.astype(bf16)

    project(info[1], own, other, own_w, first_w, second_w, store)


def near_kernel(
    info, first_att, second_att, own_w, first_w, second_w, up_low, up_high, down_low, down_high, own_out
):
    picked = [
        pick_attended(info[0], first_att, second_att, token_block(info[3], shift))
        for shift in (1, 3, 0)
    ]
    own = jnp.concatenate([p[0] for p in picked], axis=0)
    other = jnp.concatenate([p[1] for p in picked], axis=0)

    def store(half, rows, term):
        up, down = ((up_low, down_low), (up_high, down_high))[half]
        up[rows, :] = term[:, :TOK].astype(up.dtype)
        down[rows, :] = term[:, TOK : 2 * TOK].astype(down.dtype)
        own_out[slice(half * HALF + rows.start, half * HALF + rows.stop), :] = term[:, 2 * TOK :]

    project(info[1], own, other, own_w, first_w, second_w, store)


def stage_kernel(info, gate_w, up_w, down_w, ready, gate_out, up_out, down_out, sems):
    own_rows = pl.ds(pl.multiple_of(info[1] * HALF, 32), HALF)
    copies = [
        pltpu.make_async_copy(gate_w, gate_out, sems.at[0]),
        pltpu.make_async_copy(up_w, up_out, sems.at[1]),
        pltpu.make_async_copy(down_w.at[own_rows, :], down_out, sems.at[2]),
    ]
    for copy in copies:
        copy.start()
    for copy in copies:
        copy.wait()


def norm_kernel(
    info,
    own_part,
    low_a,
    low_b,
    high_a,
    high_b,
    hidden,
    gain,
    router,
    ids,
    residual_out,
    own_out,
    send_out,
    share_out,
    normed,
    held,
    sems,
):
    core = info[1]
    copies = [
        pltpu.make_async_copy(ref, held.at[n], sems.at[n])
        for n, ref in enumerate((low_a, low_b, high_a, high_b))
    ]
    for copy in copies:
        copy.start()
    for copy in copies:
        copy.wait()
    square = jnp.zeros((1, TOK), f32)
    for half in range(2):
        for lo in range(0, HALF, PART):
            rows = slice(half * HALF + lo, half * HALF + lo + PART)
            acc = hidden[rows, :].astype(f32) + own_part[rows, :]
            acc = acc + held[2 * half, lo : lo + PART, :].astype(f32)
            acc = acc + held[2 * half + 1, lo : lo + PART, :].astype(f32)
            rounded = acc.astype(bf16)
            residual_out[rows, :] = rounded
            res = rounded.astype(f32)
            square = square + jnp.sum(res * res, axis=0, keepdims=True)
    factor = lax.rsqrt(square * (1.0 / D) + norm_eps)
    for lo in range(0, D, PART):
        rows = slice(lo, lo + PART)
        res = residual_out[rows, :].astype(f32)
        normed[rows, :] = (res * factor * gain[rows, :].astype(f32)).astype(bf16)
    logits = jnp.dot(router[...], normed[...], preferred_element_type=f32)
    named = named_of(ids[...])
    raised = jnp.where(named, jnp.exp(logits), 0.0)
    share_out[...] = raised / jnp.sum(raised, axis=0, keepdims=True)
    own_out[...] = normed[pl.ds(pl.multiple_of(core * HALF, 32), HALF), :]
    send_out[:HALF, :] = normed[pl.ds(pl.multiple_of((1 - core) * HALF, 32), HALF), :]
    send_out[HALF:, :] = jnp.concatenate(
        [ids[...].astype(f32), jnp.zeros((16 - TOP, TOK), f32)], axis=0
    ).astype(bf16)


def named_of(ids):
    expert = lax.broadcasted_iota(jnp.int32, (EXPERTS, TOK), 0)
    named = expert == ids[0:1, :]
    for k in range(1, TOP):
        named = named | (expert == ids[k : k + 1, :])
    return named


def slots_of(ids, offset):
    named = named_of(ids)
    before = lax.broadcasted_iota(jnp.int32, (TOK, TOK), 0) < lax.broadcasted_iota(
        jnp.int32, (TOK, TOK), 1
    )
    rank = jnp.dot(
        named.astype(f32).astype(bf16), before.astype(f32).astype(bf16), preferred_element_type=f32
    )
    return jnp.where(named, rank + offset, -1.0)


def slot_rows(core, own_ids, other):
    start = (core * CAP).astype(f32)
    other_ids = other[HALF:, :].astype(f32).astype(jnp.int32)
    return slots_of(own_ids[...], start), slots_of(other_ids, CAP - start)


def widened(rows):
    return jnp.concatenate([rows, jnp.zeros((rows.shape[0], WIDE - HALF), rows.dtype)], axis=1)


EXPERT_BLOCK = 16
ROW_BLOCK = EXPERT_BLOCK * PAIR_ROWS


def dispatch_kernel(info, own, other, own_ids, out, slots):
    slots[:, 0:TOK], slots[:, TOK : 2 * TOK] = slot_rows(info[1], own_ids, other)
    tokens = jnp.concatenate([own[...], other[:HALF, :]], axis=1)
    place = lax.broadcasted_iota(jnp.int32, (EXPERT_BLOCK, PAIR_ROWS, 2 * TOK), 1).astype(f32)
    for n in range(EXPERTS // EXPERT_BLOCK):
        block = slots[n * EXPERT_BLOCK : (n + 1) * EXPERT_BLOCK, :]
        hit = block[:, None, :] == place
        pick = jnp.where(hit, 1.0, 0.0).reshape(ROW_BLOCK, 2 * TOK).astype(bf16)
        rows = lax.dot_general(pick, tokens, NT, preferred_element_type=f32).astype(bf16)
        out[n * ROW_BLOCK : (n + 1) * ROW_BLOCK, :] = widened(rows)


def mixing_kernel(info, own_ids, other, own_share, other_share, out):
    own_slot, other_slot = slot_rows(info[1], own_ids, other)
    slot = jnp.concatenate([own_slot, other_slot], axis=1).T.astype(bf16)
    share = jnp.concatenate([own_share[...], other_share[...]], axis=1).T
    high = share.astype(bf16)
    rest = (share - high.astype(f32)).astype(bf16)
    expert = lax.broadcasted_iota(jnp.int32, (EXPERTS, ROWS), 0) * PAIR_ROWS
    offset = lax.broadcasted_iota(jnp.int32, (EXPERTS, ROWS), 1) - expert
    inside = (offset >= 0) & (offset < PAIR_ROWS)
    spread = jnp.where(inside, 1.0, 0.0).astype(bf16)
    place = jnp.sum(jnp.where(inside, offset.astype(f32), 0.0), axis=0, keepdims=True)
    hit = jnp.dot(slot, spread, preferred_element_type=f32) == place
    for part, factor in enumerate((high, rest)):
        wide = jnp.dot(factor, spread, preferred_element_type=f32)
        out[part * 2 * TOK : (part + 1) * 2 * TOK, :] = jnp.where(hit, wide, 0.0).astype(bf16)


def active_kernel(info, own, other, gate_w, up_w, out):
    core = info[1]
    own_rows = pl.ds(pl.multiple_of(core * HALF, 32), HALF)
    other_rows = pl.ds(pl.multiple_of((1 - core) * HALF, 32), HALF)
    x_own = own[:, :HALF]
    x_other = other[:, :HALF]
    gate = jnp.dot(x_own, gate_w[own_rows, :], preferred_element_type=f32)
    gate += jnp.dot(x_other, gate_w[other_rows, :], preferred_element_type=f32)
    up = jnp.dot(x_own, up_w[own_rows, :], preferred_element_type=f32)
    up += jnp.dot(x_other, up_w[other_rows, :], preferred_element_type=f32)
    out[...] = (gate * jax.nn.sigmoid(swiglu_alpha * gate) * (up + 1.0)).astype(bf16)


def down_kernel(starts, info, *refs):
    count = len(starts)
    own, other = refs[:count], refs[count : 2 * count]
    down_w, other_w = refs[2 * count : 2 * count + 2]
    out, held, sems = refs[-3:]
    copies = []
    for n, start in enumerate(starts):
        rows = own[n].shape[0]
        first = lax.dot_general(own[n][...], down_w[...], NT, preferred_element_type=f32)
        second = lax.dot_general(other[n][...], other_w[...], NT, preferred_element_type=f32)
        both = first.astype(bf16).astype(f32) + second.astype(bf16).astype(f32)
        held[n, :rows, :] = widened(both.astype(bf16))
        copy = pltpu.make_async_copy(
            held.at[n, pl.ds(0, rows)], out.at[pl.ds(start, rows)], sems.at[n]
        )
        copy.start()
        copies.append(copy)
    for copy in copies:
        copy.wait()


MIX_BLOCK = 512


def mix_kernel(factors, rows, own_out, send_out):
    both = jnp.dot(factors[...], rows[...], preferred_element_type=f32)
    total = both[: 2 * TOK] + both[2 * TOK :]
    own_out[...] = total[:TOK].T
    send_out[...] = total[TOK:].T


def final_kernel(info, residual, own, other, out):
    core = info[1]
    for half, ref in ((core, own), (1 - core, other)):
        for lo in range(0, HALF, PART):
            rows = pl.ds(pl.multiple_of(half * HALF + lo, 32), PART)
            mix = ref[lo : lo + PART, :]
            out[rows, :] = (residual[rows, :].astype(f32) + mix).astype(bf16)


def params(mib):
    return pltpu.CompilerParams(vmem_limit_bytes=mib << 20)


def kernel_call(body, outs, operands, with_info=True, scratch=(), mib=40, flops=0, moved=0, remain=()):
    single = not isinstance(outs, list)
    specs = [SMEM_SPEC] * int(with_info) + [VMEM_SPEC] * (len(operands) - int(with_info))
    for n in remain:
        specs[n] = ANY_SPEC
    return pl.pallas_call(
        body,
        out_shape=outs,
        in_specs=specs,
        out_specs=VMEM_SPEC if single else [VMEM_SPEC] * len(outs),
        scratch_shapes=list(scratch),
        compiler_params=params(mib),
        cost_estimate=pl.CostEstimate(flops=flops, bytes_accessed=moved, transcendentals=0),
    )(*operands)


def shape(*dims, dtype=bf16):
    return jax.ShapeDtypeStruct(dims, dtype)


def local(
    hidden_in,
    queries,
    key_heads,
    values,
    doc_lengths,
    out_weight,
    norm_gain,
    router_weight,
    expert_ids,
    gate_weight,
    up_weight,
    down_weight,
):
    upper = lax.axis_index("xh")
    core = lax.axis_index("c")
    depth = lax.axis_index("z")
    info = jnp.stack([upper, core, doc_lengths[0], depth]).astype(jnp.int32)
    swap = [(0, 1), (1, 0)]

    own_w = out_weight.T
    half_w = lax.dynamic_slice_in_dim(own_w, core * HALF, HALF, axis=0)
    q, half_w = lax.optimization_barrier((queries[0], half_w))
    prepared = kernel_call(
        prepare_kernel, shape(4, TOK, 1280), (q, key_heads[0], values[0]), with_info=False
    )
    first_w = lax.ppermute(half_w, ("xh", "xl"), [(0, 3), (3, 0), (1, 2), (2, 1)])
    qkv = lax.all_to_all(prepared, "z", split_axis=0, concat_axis=0, tiled=True).reshape(512, 1280)
    lower = lax.ppermute(qkv[:, 1024:], "xh", [(0, 1)])
    down_w, qkv = lax.optimization_barrier((down_weight[0].T, qkv))
    other_down = lax.ppermute(
        lax.dynamic_slice_in_dim(down_w, (1 - core) * HALF, HALF, axis=0), "c", swap
    )

    ids = expert_ids[0].T

    def attend(a, qkv):
        return kernel_call(
            functools.partial(attention_kernel, a),
            shape(512, 512),
            (info, qkv, lower),
            scratch=(pltpu.VMEM((2, 1024, 256), bf16),) * 2,
            flops=1000,
            mib=16,
        )

    first_att = attend(0, qkv)
    first_w, first_att, qkv = lax.optimization_barrier((first_w, first_att, qkv))
    second_w = lax.ppermute(first_w, "c", swap)
    second_att = attend(1, qkv)

    plus = [(i, (i + 1) % 4) for i in range(4)]
    minus = [(i, (i + 3) % 4) for i in range(4)]
    weights = (own_w, first_w, second_w)
    half_shape = shape(HALF, TOK)
    half_float = shape(HALF, TOK, dtype=f32)
    far_low, far_high = kernel_call(
        far_kernel,
        [half_shape] * 2,
        (info, first_att, second_att) + weights,
        flops=10**9,
        mib=12,
    )

    far_low = lax.ppermute(far_low, "z", plus)
    far_high = lax.ppermute(far_high, "z", minus)
    up_low, up_high, down_low, down_high, own_part = kernel_call(
        near_kernel,
        [half_float, half_shape, half_shape, half_float, shape(D, TOK, dtype=f32)],
        (info, first_att, second_att) + weights,
        flops=2 * 10**10,
        mib=16,
    )
    high_a = lax.ppermute(up_high, "z", plus)
    low_b = lax.ppermute(down_low, "z", minus)
    relayed = (up_low + far_low.astype(f32)).astype(bf16)
    low_a = lax.ppermute(relayed, "z", plus)
    high_b = lax.ppermute((down_high + far_high.astype(f32)).astype(bf16), "z", minus)

    gate_v, up_v, down_v = pl.pallas_call(
        stage_kernel,
        out_shape=[pltpu.VMEM((D, FF), bf16)] * 2 + [pltpu.VMEM((HALF, FF), bf16)],
        in_specs=[SMEM_SPEC] + [HBM_SPEC] * 3 + [ANY_SPEC],
        out_specs=[VMEM_SPEC] * 3,
        scratch_shapes=[DMA((3,))],
        compiler_params=params(16),
    )(info, gate_weight[0], up_weight[0], down_w, relayed)
    gain = jnp.broadcast_to(norm_gain[:, None], (D, TOK))
    gain, other_down, gate_v, up_v, down_v = lax.optimization_barrier(
        (gain, other_down, gate_v, up_v, down_v)
    )
    residual, own_half, send_half, share = kernel_call(
        norm_kernel,
        [shape(D, TOK), half_shape, shape(HALF + 16, TOK), shape(EXPERTS, TOK, dtype=f32)],
        (info, own_part, low_a, low_b, high_a, high_b, hidden_in[0].T, gain, router_weight.T, ids),
        scratch=(pltpu.VMEM((D, TOK), bf16), pltpu.VMEM((4, HALF, TOK), bf16), DMA((4,))),
        remain=(2, 3, 4, 5),
        mib=12,
    )
    other_half = lax.ppermute(send_half, "c", swap)
    other_share = lax.ppermute(share, "c", swap)

    outgoing = kernel_call(
        dispatch_kernel,
        shape(ROWS, WIDE),
        (info, own_half, other_half, ids),
        scratch=(pltpu.VMEM((EXPERTS, 2 * TOK), f32),),
        mib=16,
    )
    factors = kernel_call(
        mixing_kernel,
        shape(4 * TOK, ROWS),
        (info, ids, other_half, share, other_share),
        mib=16,
    )
    chips = ("xh", "z", "xl", "y")

    def across(rows):
        return lax.all_to_all(
            rows.reshape(EXPERTS, PAIR_ROWS, WIDE), chips, split_axis=0, concat_axis=0, tiled=True
        ).reshape(ROWS, WIDE)

    arrived = across(outgoing)
    own_active, other_active = [], []
    for start, count in STEPS:
        rows = arrived[start : start + count]
        if len(own_active) == 1:
            rows, rows_other = lax.optimization_barrier((rows, rows_other))
        elif own_active:
            rows, rows_other, own_active[0] = lax.optimization_barrier(
                (rows, rows_other, own_active[0])
            )
        rows_other = lax.ppermute(rows, "c", swap)
        if len(own_active) == 2:
            rows_other, other_active[0] = lax.optimization_barrier((rows_other, other_active[0]))
        active = kernel_call(
            active_kernel,
            shape(count, FF),
            (info, rows, rows_other, gate_v, up_v),
            flops=45 * 10**8,
            mib=20,
        )
        own_active.append(active)
        other_active.append(lax.ppermute(active, "c", swap))

    def down(steps, *buffer):
        picked = [own_active[n] for n in steps] + [other_active[n] for n in steps]
        rows = max(STEPS[n][1] for n in steps)
        operands = (info, *picked, down_v, other_down, *buffer)
        return pl.pallas_call(
            functools.partial(down_kernel, [STEPS[n][0] for n in steps]),
            out_shape=pltpu.HBM((ROWS, WIDE), bf16),
            in_specs=[SMEM_SPEC] + [VMEM_SPEC] * (len(picked) + 2) + [ANY_SPEC] * len(buffer),
            out_specs=HBM_SPEC,
            scratch_shapes=[pltpu.VMEM((len(steps), rows, WIDE), bf16), DMA((len(steps),))],
            input_output_aliases={len(operands) - 1: 0} if buffer else {},
            compiler_params=params(24),
        )(*operands)

    expert_out = down([2], down([0, 1]))
    own_mix, send_mix = pl.pallas_call(
        mix_kernel,
        grid=(WIDE // MIX_BLOCK,),
        out_shape=[shape(WIDE, TOK, dtype=f32)] * 2,
        in_specs=[
            pl.BlockSpec((4 * TOK, ROWS), lambda i: (0, 0)),
            pl.BlockSpec((ROWS, MIX_BLOCK), lambda i: (0, i)),
        ],
        out_specs=[pl.BlockSpec((MIX_BLOCK, TOK), lambda i: (i, 0))] * 2,
        compiler_params=params(32),
    )(factors, across(expert_out))
    other_mix = lax.ppermute(send_mix, "c", swap)
    layer_out = kernel_call(
        final_kernel, shape(D, TOK), (info, residual, own_mix, other_mix), mib=12
    )
    return layer_out.T[None]


def solution(mesh):
    split_mesh = Mesh(mesh.devices.reshape(2, 4, 2, 4, 2), ("xh", "z", "xl", "y", "c"))
    seq = ("xh", "z")
    doc = ("xl", "y", "c")
    in_specs = (
        P(doc, seq, None),
        P(doc, seq, None),
        P(doc, seq, None),
        P(doc, seq, None),
        P(doc),
        P(seq, None),
        P(),
        P(),
        P(doc, seq, None),
        P(seq + doc, None, None),
        P(seq + doc, None, None),
        P(seq + doc, None, None),
    )
    return jax.shard_map(
        local,
        mesh=split_mesh,
        in_specs=in_specs,
        out_specs=P(doc, seq, None),
        check_vma=False,
    )
```

```python
import functools
import jax
import jax.numpy as jnp
from jax import lax
from jax.experimental import pallas as pl
from jax.experimental.pallas import tpu as pltpu
from jax.sharding import Mesh, PartitionSpec as P

HD = 64
TOP = 4
EXPERTS = 64
TOK = 128
D = 2880
FF = 768
HALF = D // 2
WIDE = 1536
CAP = 12
PAIR_ROWS = 2 * CAP
ROWS = EXPERTS * PAIR_ROWS
PART = 480
STEPS = ((0, 256), (256, 640), (896, 640))

negative_fill = -1e30
swiglu_alpha = 1.702
norm_eps = 1e-05
exp_scale = HD ** (-0.5) * 1.4426950408889634

f32 = jnp.float32
bf16 = jnp.bfloat16
VMEM_SPEC = pl.BlockSpec(memory_space=pltpu.VMEM)
SMEM_SPEC = pl.BlockSpec(memory_space=pltpu.SMEM)
HBM_SPEC = pl.BlockSpec(memory_space=pltpu.HBM)
ANY_SPEC = pl.BlockSpec(memory_space=pl.ANY)
DMA = pltpu.SemaphoreType.DMA
NT = (((1,), (1,)), ((), ()))


def prepare_kernel(queries, key_heads, values, out):
    lane = lax.broadcasted_iota(jnp.int32, (TOK, 128), 1)
    for z in range(4):
        out[z, :, 0:512] = queries[:, z * 512 : z * 512 + 512]
        out[z, :, 512:1024] = queries[:, 2048 + z * 512 : 2560 + z * 512]
        tile = (z // 2) * 128
        for n, ref in enumerate((key_heads, values)):
            first = ref[:, tile : tile + 128].astype(f32)
            second = ref[:, 256 + tile : 384 + tile].astype(f32)
            if z % 2 == 0:
                second = pltpu.roll(second, 64, 1)
            else:
                first = pltpu.roll(first, 64, 1)
            out[z, :, 1024 + 128 * n : 1152 + 128 * n] = jnp.where(
                lane < 64, first, second
            ).astype(bf16)


def attention_kernel(a, info, qkv, lower_ref, att, keys, vals, lower, sem):
    upper = info[0]
    doc_len = info[2]
    fetch = pltpu.make_async_copy(lower_ref, lower, sem)
    fetch.start()
    fetch.wait()
    lane = lax.broadcasted_iota(jnp.int32, (512, 128), 1)
    low = lane < 64
    one = jnp.ones((512, 128), f32)
    row = lax.broadcasted_iota(jnp.int32, (512, 128), 0)
    for side in range(2):
        rows = pl.ds(512 * side, 512)
        source = qkv[:, 1024:1280] if side else lower[...]
        kk = source[:, 0:128].astype(f32)
        vv = source[:, 128:256].astype(f32)
        kr = pltpu.roll(kk, 64, 1)
        vr = pltpu.roll(vv, 64, 1)
        position = row + 512 * upper if side else row
        masked = (lane == 0) & (position >= doc_len)
        bias = jnp.where(masked, negative_fill, 0.0).astype(bf16)
        for par in range(2):
            keep = low if par == 0 else ~low
            keys[par, rows, 0:128] = jnp.where(keep, kk if a == par else kr, 0.0).astype(bf16)
            keys[par, rows, 128:256] = bias
            vals[par, rows, 0:128] = jnp.where(keep, vv if a == par else vr, 0.0).astype(bf16)
            vals[par, rows, 128:256] = jnp.where(keep, one, 0.0).astype(bf16)

    first_lane = jnp.where(lane == 0, 1.0, 0.0).astype(bf16)
    causal = jnp.where(
        lax.broadcasted_iota(jnp.int32, (128, 128), 1)
        <= lax.broadcasted_iota(jnp.int32, (128, 128), 0),
        0.0,
        negative_fill,
    )
    causal = jnp.concatenate([causal] * 4, axis=0)

    def block(i, with_other):
        nk = (i + 1) * 128 + (512 if with_other else 0)
        start = 0 if with_other else 512
        q_rows = slice(i * 128, (i + 1) * 128)
        q_tiles = [qkv[q_rows, a * 512 + 128 * t : a * 512 + 128 * (t + 1)] for t in range(4)]
        q_stack = jnp.concatenate([jnp.concatenate(q_tiles, axis=0), first_lane], axis=1)
        total = None
        for par in range(2):
            k_blk = keys[par, start : start + nk, :]
            scores = lax.dot_general(q_stack, k_blk, NT, preferred_element_type=f32)
            last = scores[:, nk - 128 :] + causal
            if nk > 128:
                scores = jnp.concatenate([scores[:, : nk - 128], last], axis=1)
            else:
                scores = last
            top = jnp.max(scores, axis=1, keepdims=True)
            weights = jnp.exp2((scores - top) * exp_scale).astype(bf16)
            part = jnp.dot(
                weights, vals[par, start : start + nk, :], preferred_element_type=f32
            )
            total = part if total is None else total + part
        result = (total[:, 0:128] / total[:, 128:256]).astype(bf16)
        for t in range(4):
            att[q_rows, 128 * t : 128 * (t + 1)] = result[128 * t : 128 * (t + 1)]

    @pl.when(upper == 1)
    def _():
        for i in range(4):
            block(i, True)

    @pl.when(upper == 0)
    def _():
        for i in range(4):
            block(i, False)


def pick_attended(upper, first_att, second_att, rows):
    first, second = first_att[rows, :], second_att[rows, :]
    return jnp.where(upper == 0, first, second), jnp.where(upper == 0, second, first)


def project(core, own, other, own_w, first_w, second_w, store):
    for half in range(2):
        for lo in range(0, HALF, PART):
            rows = slice(half * HALF + lo, half * HALF + lo + PART)
            far = slice(lo, lo + PART)
            far_w = jnp.where(core == half, first_w[far, :], second_w[far, :])
            term = lax.dot_general(own_w[rows, :], own, NT, preferred_element_type=f32)
            term += lax.dot_general(far_w, other, NT, preferred_element_type=f32)
            store(half, far, term)


def token_block(z, shift):
    return pl.ds(pl.multiple_of(lax.rem(z + shift, 4) * TOK, TOK), TOK)


def far_kernel(info, first_att, second_att, own_w, first_w, second_w, low_out, high_out):
    own, other = pick_attended(info[0], first_att, second_att, token_block(info[3], 2))

    def store(half, rows, term):
        (low_out, high_out)[half][rows, :] = term.astype(bf16)

    project(info[1], own, other, own_w, first_w, second_w, store)


def near_kernel(
    info, first_att, second_att, own_w, first_w, second_w, up_low, up_high, down_low, down_high, own_out
):
    picked = [
        pick_attended(info[0], first_att, second_att, token_block(info[3], shift))
        for shift in (1, 3, 0)
    ]
    own = jnp.concatenate([p[0] for p in picked], axis=0)
    other = jnp.concatenate([p[1] for p in picked], axis=0)

    def store(half, rows, term):
        up, down = ((up_low, down_low), (up_high, down_high))[half]
        up[rows, :] = term[:, :TOK].astype(up.dtype)
        down[rows, :] = term[:, TOK : 2 * TOK].astype(down.dtype)
        own_out[slice(half * HALF + rows.start, half * HALF + rows.stop), :] = term[:, 2 * TOK :]

    project(info[1], own, other, own_w, first_w, second_w, store)


def stage_kernel(info, gate_w, up_w, down_w, ready, gate_out, up_out, down_out, send_out, sems):
    own_rows = pl.ds(pl.multiple_of(info[1] * HALF, 32), HALF)
    other_rows = pl.ds(pl.multiple_of((1 - info[1]) * HALF, 32), HALF)
    copies = [
        pltpu.make_async_copy(down_w.at[other_rows, :], send_out, sems.at[3]),
        pltpu.make_async_copy(gate_w, gate_out, sems.at[0]),
        pltpu.make_async_copy(up_w, up_out, sems.at[1]),
        pltpu.make_async_copy(down_w.at[own_rows, :], down_out, sems.at[2]),
    ]
    for copy in copies:
        copy.start()
    for copy in copies:
        copy.wait()


def norm_kernel(
    info,
    own_part,
    low_a,
    low_b,
    high_a,
    high_b,
    hidden,
    gain,
    router,
    ids,
    residual_out,
    own_out,
    send_out,
    share_out,
    normed,
    held,
    sems,
):
    core = info[1]
    copies = [
        pltpu.make_async_copy(ref, held.at[n], sems.at[n])
        for n, ref in enumerate((low_a, low_b, high_a, high_b))
    ]
    for copy in copies:
        copy.start()
    for copy in copies:
        copy.wait()
    square = jnp.zeros((1, TOK), f32)
    for half in range(2):
        for lo in range(0, HALF, PART):
            rows = slice(half * HALF + lo, half * HALF + lo + PART)
            acc = hidden[rows, :].astype(f32) + own_part[rows, :]
            acc = acc + held[2 * half, lo : lo + PART, :].astype(f32)
            acc = acc + held[2 * half + 1, lo : lo + PART, :].astype(f32)
            rounded = acc.astype(bf16)
            residual_out[rows, :] = rounded
            res = rounded.astype(f32)
            square = square + jnp.sum(res * res, axis=0, keepdims=True)
    factor = lax.rsqrt(square * (1.0 / D) + norm_eps)
    for lo in range(0, D, PART):
        rows = slice(lo, lo + PART)
        res = residual_out[rows, :].astype(f32)
        normed[rows, :] = (res * factor * gain[rows, :].astype(f32)).astype(bf16)
    logits = jnp.dot(router[...], normed[...], preferred_element_type=f32)
    named = named_of(ids[...])
    raised = jnp.where(named, jnp.exp(logits), 0.0)
    share_out[...] = raised / jnp.sum(raised, axis=0, keepdims=True)
    own_out[...] = normed[pl.ds(pl.multiple_of(core * HALF, 32), HALF), :]
    send_out[:HALF, :] = normed[pl.ds(pl.multiple_of((1 - core) * HALF, 32), HALF), :]
    send_out[HALF:, :] = jnp.concatenate(
        [ids[...].astype(f32), jnp.zeros((16 - TOP, TOK), f32)], axis=0
    ).astype(bf16)


def named_of(ids):
    expert = lax.broadcasted_iota(jnp.int32, (EXPERTS, TOK), 0)
    named = expert == ids[0:1, :]
    for k in range(1, TOP):
        named = named | (expert == ids[k : k + 1, :])
    return named


def slots_of(ids, offset):
    named = named_of(ids)
    before = lax.broadcasted_iota(jnp.int32, (TOK, TOK), 0) < lax.broadcasted_iota(
        jnp.int32, (TOK, TOK), 1
    )
    rank = jnp.dot(
        named.astype(f32).astype(bf16), before.astype(f32).astype(bf16), preferred_element_type=f32
    )
    return jnp.where(named, rank + offset, -1.0)


def slot_rows(core, own_ids, other):
    start = (core * CAP).astype(f32)
    other_ids = other[HALF:, :].astype(f32).astype(jnp.int32)
    return slots_of(own_ids[...], start), slots_of(other_ids, CAP - start)


def widened(rows):
    return jnp.concatenate([rows, jnp.zeros((rows.shape[0], WIDE - HALF), rows.dtype)], axis=1)


EXPERT_BLOCK = 16
ROW_BLOCK = EXPERT_BLOCK * PAIR_ROWS


def dispatch_kernel(info, own, other, own_ids, out, slots):
    slots[:, 0:TOK], slots[:, TOK : 2 * TOK] = slot_rows(info[1], own_ids, other)
    tokens = jnp.concatenate([own[...], other[:HALF, :]], axis=1)
    place = lax.broadcasted_iota(jnp.int32, (EXPERT_BLOCK, PAIR_ROWS, 2 * TOK), 1).astype(f32)
    for n in range(EXPERTS // EXPERT_BLOCK):
        block = slots[n * EXPERT_BLOCK : (n + 1) * EXPERT_BLOCK, :]
        hit = block[:, None, :] == place
        pick = jnp.where(hit, 1.0, 0.0).reshape(ROW_BLOCK, 2 * TOK).astype(bf16)
        rows = lax.dot_general(pick, tokens, NT, preferred_element_type=f32).astype(bf16)
        out[n * ROW_BLOCK : (n + 1) * ROW_BLOCK, :] = widened(rows)


def mixing_kernel(info, own_ids, other, own_share, other_share, out):
    own_slot, other_slot = slot_rows(info[1], own_ids, other)
    slot = jnp.concatenate([own_slot, other_slot], axis=1).T.astype(bf16)
    share = jnp.concatenate([own_share[...], other_share[...]], axis=1).T
    high = share.astype(bf16)
    rest = (share - high.astype(f32)).astype(bf16)
    expert = lax.broadcasted_iota(jnp.int32, (EXPERTS, ROWS), 0) * PAIR_ROWS
    offset = lax.broadcasted_iota(jnp.int32, (EXPERTS, ROWS), 1) - expert
    inside = (offset >= 0) & (offset < PAIR_ROWS)
    spread = jnp.where(inside, 1.0, 0.0).astype(bf16)
    place = jnp.sum(jnp.where(inside, offset.astype(f32), 0.0), axis=0, keepdims=True)
    hit = jnp.dot(slot, spread, preferred_element_type=f32) == place
    for part, factor in enumerate((high, rest)):
        wide = jnp.dot(factor, spread, preferred_element_type=f32)
        out[part * 2 * TOK : (part + 1) * 2 * TOK, :] = jnp.where(hit, wide, 0.0).astype(bf16)


def active_kernel(info, own, other, gate_w, up_w, out):
    core = info[1]
    own_rows = pl.ds(pl.multiple_of(core * HALF, 32), HALF)
    other_rows = pl.ds(pl.multiple_of((1 - core) * HALF, 32), HALF)
    x_own = own[:, :HALF]
    x_other = other[:, :HALF]
    gate = jnp.dot(x_own, gate_w[own_rows, :], preferred_element_type=f32)
    gate += jnp.dot(x_other, gate_w[other_rows, :], preferred_element_type=f32)
    up = jnp.dot(x_own, up_w[own_rows, :], preferred_element_type=f32)
    up += jnp.dot(x_other, up_w[other_rows, :], preferred_element_type=f32)
    out[...] = (gate * jax.nn.sigmoid(swiglu_alpha * gate) * (up + 1.0)).astype(bf16)


def down_kernel(starts, info, *refs):
    count = len(starts)
    own, other = refs[:count], refs[count : 2 * count]
    down_w, other_w = refs[2 * count : 2 * count + 2]
    out = refs[-1]
    for n, start in enumerate(starts):
        first = lax.dot_general(own[n][...], down_w[...], NT, preferred_element_type=f32)
        second = lax.dot_general(other[n][...], other_w[...], NT, preferred_element_type=f32)
        both = first.astype(bf16).astype(f32) + second.astype(bf16).astype(f32)
        out[start : start + own[n].shape[0], :] = widened(both.astype(bf16))


MIX_BLOCK = 512


def mix_kernel(factors, rows, own_out, send_out):
    both = jnp.dot(factors[...], rows[...], preferred_element_type=f32)
    total = both[: 2 * TOK] + both[2 * TOK :]
    own_out[...] = total[:TOK].T
    send_out[...] = total[TOK:].T


def final_kernel(info, residual, own, other, out):
    core = info[1]
    for half, ref in ((core, own), (1 - core, other)):
        for lo in range(0, HALF, PART):
            rows = pl.ds(pl.multiple_of(half * HALF + lo, 32), PART)
            mix = ref[lo : lo + PART, :]
            out[rows, :] = (residual[rows, :].astype(f32) + mix).astype(bf16)


def params(mib):
    return pltpu.CompilerParams(vmem_limit_bytes=mib << 20)


def kernel_call(body, outs, operands, with_info=True, scratch=(), mib=40, flops=0, moved=0, remain=()):
    single = not isinstance(outs, list)
    specs = [SMEM_SPEC] * int(with_info) + [VMEM_SPEC] * (len(operands) - int(with_info))
    for n in remain:
        specs[n] = ANY_SPEC
    return pl.pallas_call(
        body,
        out_shape=outs,
        in_specs=specs,
        out_specs=VMEM_SPEC if single else [VMEM_SPEC] * len(outs),
        scratch_shapes=list(scratch),
        compiler_params=params(mib),
        cost_estimate=pl.CostEstimate(flops=flops, bytes_accessed=moved, transcendentals=0),
    )(*operands)


def shape(*dims, dtype=bf16):
    return jax.ShapeDtypeStruct(dims, dtype)


def local(
    hidden_in,
    queries,
    key_heads,
    values,
    doc_lengths,
    out_weight,
    norm_gain,
    router_weight,
    expert_ids,
    gate_weight,
    up_weight,
    down_weight,
):
    upper = lax.axis_index("xh")
    core = lax.axis_index("c")
    depth = lax.axis_index("z")
    info = jnp.stack([upper, core, doc_lengths[0], depth]).astype(jnp.int32)
    swap = [(0, 1), (1, 0)]

    own_w = out_weight.T
    half_w = lax.dynamic_slice_in_dim(own_w, core * HALF, HALF, axis=0)
    q, half_w = lax.optimization_barrier((queries[0], half_w))
    prepared = kernel_call(
        prepare_kernel, shape(4, TOK, 1280), (q, key_heads[0], values[0]), with_info=False
    )
    first_w = lax.ppermute(half_w, ("xh", "xl"), [(0, 3), (3, 0), (1, 2), (2, 1)])
    qkv = lax.all_to_all(prepared, "z", split_axis=0, concat_axis=0, tiled=True).reshape(512, 1280)
    lower = lax.ppermute(qkv[:, 1024:], "xh", [(0, 1)])
    ids = expert_ids[0].T

    def attend(a, qkv):
        return kernel_call(
            functools.partial(attention_kernel, a),
            shape(512, 512),
            (info, qkv, lower),
            scratch=(pltpu.VMEM((2, 1024, 256), bf16),) * 2 + (pltpu.VMEM((512, 256), bf16), DMA(())),
            remain=(2,),
            flops=1000,
            mib=16,
        )

    first_att = attend(0, qkv)
    first_w, first_att, qkv = lax.optimization_barrier((first_w, first_att, qkv))
    second_w = lax.ppermute(first_w, "c", swap)
    second_att = attend(1, qkv)

    plus = [(i, (i + 1) % 4) for i in range(4)]
    minus = [(i, (i + 3) % 4) for i in range(4)]
    weights = (own_w, first_w, second_w)
    half_shape = shape(HALF, TOK)
    half_float = shape(HALF, TOK, dtype=f32)
    far_low, far_high = kernel_call(
        far_kernel,
        [half_shape] * 2,
        (info, first_att, second_att) + weights,
        flops=10**9,
        mib=12,
    )

    far_low = lax.ppermute(far_low, "z", plus)
    far_high = lax.ppermute(far_high, "z", minus)
    up_low, up_high, down_low, down_high, own_part = kernel_call(
        near_kernel,
        [half_float, half_shape, half_shape, half_float, shape(D, TOK, dtype=f32)],
        (info, first_att, second_att) + weights,
        flops=2 * 10**10,
        mib=16,
    )
    high_a = lax.ppermute(up_high, "z", plus)
    low_b = lax.ppermute(down_low, "z", minus)
    relayed = (up_low + far_low.astype(f32)).astype(bf16)
    low_a = lax.ppermute(relayed, "z", plus)
    relayed_high = (down_high + far_high.astype(f32)).astype(bf16)
    high_b = lax.ppermute(relayed_high, "z", minus)

    gate_v, up_v, down_v, send_down = pl.pallas_call(
        stage_kernel,
        out_shape=[pltpu.VMEM((D, FF), bf16)] * 2 + [pltpu.VMEM((HALF, FF), bf16)] * 2,
        in_specs=[SMEM_SPEC] + [HBM_SPEC] * 3 + [ANY_SPEC],
        out_specs=[VMEM_SPEC] * 4,
        scratch_shapes=[DMA((4,))],
        compiler_params=params(16),
    )(info, gate_weight[0], up_weight[0], down_weight[0].T, relayed)
    other_down = lax.ppermute(send_down, "c", swap)
    gain = jnp.broadcast_to(norm_gain[:, None], (D, TOK))
    gain, gate_v, up_v, down_v = lax.optimization_barrier((gain, gate_v, up_v, down_v))
    residual, own_half, send_half, share = kernel_call(
        norm_kernel,
        [shape(D, TOK), half_shape, shape(HALF + 16, TOK), shape(EXPERTS, TOK, dtype=f32)],
        (info, own_part, low_a, low_b, high_a, high_b, hidden_in[0].T, gain, router_weight.T, ids),
        scratch=(pltpu.VMEM((D, TOK), bf16), pltpu.VMEM((4, HALF, TOK), bf16), DMA((4,))),
        remain=(2, 3, 4, 5),
        mib=12,
    )
    other_half = lax.ppermute(send_half, "c", swap)
    other_share = lax.ppermute(share, "c", swap)

    outgoing = kernel_call(
        dispatch_kernel,
        shape(ROWS, WIDE),
        (info, own_half, other_half, ids),
        scratch=(pltpu.VMEM((EXPERTS, 2 * TOK), f32),),
        mib=16,
    )
    chips = ("xh", "z", "xl", "y")

    def across(rows):
        return lax.all_to_all(
            rows.reshape(EXPERTS, PAIR_ROWS, WIDE), chips, split_axis=0, concat_axis=0, tiled=True
        ).reshape(ROWS, WIDE)

    arrived = across(outgoing)
    arrived, share = lax.optimization_barrier((arrived, share))
    factors = kernel_call(
        mixing_kernel,
        shape(4 * TOK, ROWS),
        (info, ids, other_half, share, other_share),
        mib=16,
    )
    own_active, other_active = [], []
    for start, count in STEPS:
        rows = arrived[start : start + count]
        if len(own_active) == 1:
            rows, rows_other = lax.optimization_barrier((rows, rows_other))
        elif own_active:
            rows, rows_other, own_active[0] = lax.optimization_barrier(
                (rows, rows_other, own_active[0])
            )
        rows_other = lax.ppermute(rows, "c", swap)
        if not own_active:
            rows_other, factors = lax.optimization_barrier((rows_other, factors))
        if len(own_active) == 2:
            rows_other, other_active[0] = lax.optimization_barrier((rows_other, other_active[0]))
        active = kernel_call(
            active_kernel,
            shape(count, FF),
            (info, rows, rows_other, gate_v, up_v),
            flops=45 * 10**8,
            mib=20,
        )
        own_active.append(active)
        other_active.append(lax.ppermute(active, "c", swap))

    def down(steps, *buffer):
        picked = [own_active[n] for n in steps] + [other_active[n] for n in steps]
        operands = (info, *picked, down_v, other_down, *buffer)
        return pl.pallas_call(
            functools.partial(down_kernel, [STEPS[n][0] for n in steps]),
            out_shape=shape(ROWS, WIDE),
            in_specs=[SMEM_SPEC] + [VMEM_SPEC] * (len(operands) - 1),
            out_specs=VMEM_SPEC,
            input_output_aliases={len(operands) - 1: 0} if buffer else {},
            compiler_params=params(24),
        )(*operands)

    expert_out = down([2], down([0, 1]))
    own_mix, send_mix = pl.pallas_call(
        mix_kernel,
        grid=(WIDE // MIX_BLOCK,),
        out_shape=[shape(WIDE, TOK, dtype=f32)] * 2,
        in_specs=[
            pl.BlockSpec((4 * TOK, ROWS), lambda i: (0, 0)),
            pl.BlockSpec((ROWS, MIX_BLOCK), lambda i: (0, i)),
        ],
        out_specs=[pl.BlockSpec((MIX_BLOCK, TOK), lambda i: (i, 0))] * 2,
        compiler_params=params(32),
    )(factors, across(expert_out))
    other_mix = lax.ppermute(send_mix, "c", swap)
    layer_out = kernel_call(
        final_kernel, shape(D, TOK), (info, residual, own_mix, other_mix), mib=12
    )
    return layer_out.T[None]


def solution(mesh):
    split_mesh = Mesh(mesh.devices.reshape(2, 4, 2, 4, 2), ("xh", "z", "xl", "y", "c"))
    seq = ("xh", "z")
    doc = ("xl", "y", "c")
    in_specs = (
        P(doc, seq, None),
        P(doc, seq, None),
        P(doc, seq, None),
        P(doc, seq, None),
        P(doc),
        P(seq, None),
        P(),
        P(),
        P(doc, seq, None),
        P(seq + doc, None, None),
        P(seq + doc, None, None),
        P(seq + doc, None, None),
    )
    return jax.shard_map(
        local,
        mesh=split_mesh,
        in_specs=in_specs,
        out_specs=P(doc, seq, None),
        check_vma=False,
    )
```

```python
import functools
import jax
import jax.numpy as jnp
from jax import lax
from jax.experimental import pallas as pl
from jax.experimental.pallas import tpu as pltpu
from jax.sharding import Mesh, PartitionSpec as P

HD = 64
TOP = 4
EXPERTS = 64
TOK = 128
D = 2880
FF = 768
HALF = D // 2
WIDE = 1536
CAP = 12
PAIR_ROWS = 2 * CAP
ROWS = EXPERTS * PAIR_ROWS
PART = 480
STEPS = ((0, 256), (256, 640), (896, 640))

negative_fill = -1e30
swiglu_alpha = 1.702
norm_eps = 1e-05
exp_scale = HD ** (-0.5) * 1.4426950408889634

f32 = jnp.float32
bf16 = jnp.bfloat16
VMEM_SPEC = pl.BlockSpec(memory_space=pltpu.VMEM)
SMEM_SPEC = pl.BlockSpec(memory_space=pltpu.SMEM)
HBM_SPEC = pl.BlockSpec(memory_space=pltpu.HBM)
ANY_SPEC = pl.BlockSpec(memory_space=pl.ANY)
DMA = pltpu.SemaphoreType.DMA
NT = (((1,), (1,)), ((), ()))


def prepare_kernel(queries, key_heads, values, out):
    lane = lax.broadcasted_iota(jnp.int32, (TOK, 128), 1)
    for z in range(4):
        out[z, :, 0:512] = queries[:, z * 512 : z * 512 + 512]
        out[z, :, 512:1024] = queries[:, 2048 + z * 512 : 2560 + z * 512]
        tile = (z // 2) * 128
        for n, ref in enumerate((key_heads, values)):
            first = ref[:, tile : tile + 128].astype(f32)
            second = ref[:, 256 + tile : 384 + tile].astype(f32)
            if z % 2 == 0:
                second = pltpu.roll(second, 64, 1)
            else:
                first = pltpu.roll(first, 64, 1)
            out[z, :, 1024 + 128 * n : 1152 + 128 * n] = jnp.where(
                lane < 64, first, second
            ).astype(bf16)


def attention_kernel(a, info, qkv, lower_ref, att, keys, vals, lower, sem):
    upper = info[0]
    doc_len = info[2]
    fetch = pltpu.make_async_copy(lower_ref, lower, sem)
    fetch.start()
    fetch.wait()
    lane = lax.broadcasted_iota(jnp.int32, (512, 128), 1)
    low = lane < 64
    one = jnp.ones((512, 128), f32)
    row = lax.broadcasted_iota(jnp.int32, (512, 128), 0)
    for side in range(2):
        rows = pl.ds(512 * side, 512)
        source = qkv[:, 1024:1280] if side else lower[...]
        kk = source[:, 0:128].astype(f32)
        vv = source[:, 128:256].astype(f32)
        kr = pltpu.roll(kk, 64, 1)
        vr = pltpu.roll(vv, 64, 1)
        position = row + 512 * upper if side else row
        masked = (lane == 0) & (position >= doc_len)
        bias = jnp.where(masked, negative_fill, 0.0).astype(bf16)
        for par in range(2):
            keep = low if par == 0 else ~low
            keys[par, rows, 0:128] = jnp.where(keep, kk if a == par else kr, 0.0).astype(bf16)
            keys[par, rows, 128:256] = bias
            vals[par, rows, 0:128] = jnp.where(keep, vv if a == par else vr, 0.0).astype(bf16)
            vals[par, rows, 128:256] = jnp.where(keep, one, 0.0).astype(bf16)

    first_lane = jnp.where(lane == 0, 1.0, 0.0).astype(bf16)
    causal = jnp.where(
        lax.broadcasted_iota(jnp.int32, (128, 128), 1)
        <= lax.broadcasted_iota(jnp.int32, (128, 128), 0),
        0.0,
        negative_fill,
    )
    causal = jnp.concatenate([causal] * 4, axis=0)

    def block(i, with_other):
        nk = (i + 1) * 128 + (512 if with_other else 0)
        start = 0 if with_other else 512
        q_rows = slice(i * 128, (i + 1) * 128)
        q_tiles = [qkv[q_rows, a * 512 + 128 * t : a * 512 + 128 * (t + 1)] for t in range(4)]
        q_stack = jnp.concatenate([jnp.concatenate(q_tiles, axis=0), first_lane], axis=1)
        total = None
        for par in range(2):
            k_blk = keys[par, start : start + nk, :]
            scores = lax.dot_general(q_stack, k_blk, NT, preferred_element_type=f32)
            last = scores[:, nk - 128 :] + causal
            if nk > 128:
                scores = jnp.concatenate([scores[:, : nk - 128], last], axis=1)
            else:
                scores = last
            top = jnp.max(scores, axis=1, keepdims=True)
            weights = jnp.exp2((scores - top) * exp_scale).astype(bf16)
            part = jnp.dot(
                weights, vals[par, start : start + nk, :], preferred_element_type=f32
            )
            total = part if total is None else total + part
        result = (total[:, 0:128] / total[:, 128:256]).astype(bf16)
        for t in range(4):
            att[q_rows, 128 * t : 128 * (t + 1)] = result[128 * t : 128 * (t + 1)]

    @pl.when(upper == 1)
    def _():
        for i in range(4):
            block(i, True)

    @pl.when(upper == 0)
    def _():
        for i in range(4):
            block(i, False)


def pick_attended(upper, first_att, second_att, rows):
    first, second = first_att[rows, :], second_att[rows, :]
    return jnp.where(upper == 0, first, second), jnp.where(upper == 0, second, first)


def project(core, own, other, own_w, first_w, second_w, store):
    for half in range(2):
        for lo in range(0, HALF, PART):
            rows = slice(half * HALF + lo, half * HALF + lo + PART)
            far = slice(lo, lo + PART)
            far_w = jnp.where(core == half, first_w[far, :], second_w[far, :])
            term = lax.dot_general(own_w[rows, :], own, NT, preferred_element_type=f32)
            term += lax.dot_general(far_w, other, NT, preferred_element_type=f32)
            store(half, far, term)


def token_block(z, shift):
    return pl.ds(pl.multiple_of(lax.rem(z + shift, 4) * TOK, TOK), TOK)


def far_kernel(info, first_att, second_att, own_w, first_w, second_w, low_out, high_out):
    own, other = pick_attended(info[0], first_att, second_att, token_block(info[3], 2))

    def store(half, rows, term):
        (low_out, high_out)[half][rows, :] = term.astype(bf16)

    project(info[1], own, other, own_w, first_w, second_w, store)


def near_kernel(
    info, first_att, second_att, own_w, first_w, second_w, up_low, up_high, down_low, down_high, own_out
):
    picked = [
        pick_attended(info[0], first_att, second_att, token_block(info[3], shift))
        for shift in (1, 3, 0)
    ]
    own = jnp.concatenate([p[0] for p in picked], axis=0)
    other = jnp.concatenate([p[1] for p in picked], axis=0)

    def store(half, rows, term):
        up, down = ((up_low, down_low), (up_high, down_high))[half]
        up[rows, :] = term[:, :TOK].astype(up.dtype)
        down[rows, :] = term[:, TOK : 2 * TOK].astype(down.dtype)
        own_out[slice(half * HALF + rows.start, half * HALF + rows.stop), :] = term[:, 2 * TOK :]

    project(info[1], own, other, own_w, first_w, second_w, store)


def stage_kernel(info, gate_w, up_w, down_w, ready, gate_out, up_out, down_out, send_out, sems):
    own_rows = pl.ds(pl.multiple_of(info[1] * HALF, 32), HALF)
    other_rows = pl.ds(pl.multiple_of((1 - info[1]) * HALF, 32), HALF)
    copies = [
        pltpu.make_async_copy(down_w.at[other_rows, :], send_out, sems.at[3]),
        pltpu.make_async_copy(gate_w, gate_out, sems.at[0]),
        pltpu.make_async_copy(up_w, up_out, sems.at[1]),
        pltpu.make_async_copy(down_w.at[own_rows, :], down_out, sems.at[2]),
    ]
    for copy in copies:
        copy.start()
    for copy in copies:
        copy.wait()


def norm_kernel(
    info,
    own_part,
    low_a,
    low_b,
    high_a,
    high_b,
    hidden,
    gain,
    router,
    ids,
    residual_out,
    own_out,
    send_out,
    share_out,
    normed,
    held,
    sems,
):
    core = info[1]
    copies = [
        pltpu.make_async_copy(ref, held.at[n], sems.at[n])
        for n, ref in enumerate((low_a, low_b, high_a, high_b))
    ]
    for copy in copies:
        copy.start()
    for copy in copies:
        copy.wait()
    square = jnp.zeros((1, TOK), f32)
    for half in range(2):
        for lo in range(0, HALF, PART):
            rows = slice(half * HALF + lo, half * HALF + lo + PART)
            acc = hidden[rows, :].astype(f32) + own_part[rows, :]
            acc = acc + held[2 * half, lo : lo + PART, :].astype(f32)
            acc = acc + held[2 * half + 1, lo : lo + PART, :].astype(f32)
            rounded = acc.astype(bf16)
            residual_out[rows, :] = rounded
            res = rounded.astype(f32)
            square = square + jnp.sum(res * res, axis=0, keepdims=True)
    factor = lax.rsqrt(square * (1.0 / D) + norm_eps)
    for lo in range(0, D, PART):
        rows = slice(lo, lo + PART)
        res = residual_out[rows, :].astype(f32)
        normed[rows, :] = (res * factor * gain[rows, :].astype(f32)).astype(bf16)
    logits = jnp.dot(router[...], normed[...], preferred_element_type=f32)
    logits = jnp.concatenate(
        [logits[(xh * 4 + z) * 8 : (xh * 4 + z) * 8 + 8] for z in range(4) for xh in range(2)], axis=0
    )
    named = named_of(ids[...])
    raised = jnp.where(named, jnp.exp(logits), 0.0)
    share = raised / jnp.sum(raised, axis=0, keepdims=True)
    high = share.astype(bf16)
    share_out[:EXPERTS, :] = high
    share_out[EXPERTS:, :] = (share - high.astype(f32)).astype(bf16)
    own_out[...] = normed[pl.ds(pl.multiple_of(core * HALF, 32), HALF), :]
    send_out[:HALF, :] = normed[pl.ds(pl.multiple_of((1 - core) * HALF, 32), HALF), :]
    send_out[HALF + 16 :, :] = share_out[...]
    send_out[HALF : HALF + 16, :] = jnp.concatenate(
        [ids[...].astype(f32), jnp.zeros((16 - TOP, TOK), f32)], axis=0
    ).astype(bf16)


def named_of(ids):
    place = lax.broadcasted_iota(jnp.int32, (EXPERTS, TOK), 0)
    expert = ((place >> 3) & 1) * 32 + (place >> 4) * 8 + (place & 7)
    named = expert == ids[0:1, :]
    for k in range(1, TOP):
        named = named | (expert == ids[k : k + 1, :])
    return named


def slots_of(ids, offset):
    named = named_of(ids)
    before = lax.broadcasted_iota(jnp.int32, (TOK, TOK), 0) < lax.broadcasted_iota(
        jnp.int32, (TOK, TOK), 1
    )
    rank = jnp.dot(
        named.astype(f32).astype(bf16), before.astype(f32).astype(bf16), preferred_element_type=f32
    )
    return jnp.where(named, rank + offset, -1.0)


def slot_rows(core, own_ids, other):
    start = (core * CAP).astype(f32)
    other_ids = other[HALF : HALF + 16, :].astype(f32).astype(jnp.int32)
    return slots_of(own_ids[...], start), slots_of(other_ids, CAP - start)


def widened(rows):
    return jnp.concatenate([rows, jnp.zeros((rows.shape[0], WIDE - HALF), rows.dtype)], axis=1)


EXPERT_BLOCK = 16
ROW_BLOCK = EXPERT_BLOCK * PAIR_ROWS


def dispatch_kernel(info, own, other, own_ids, out, slots):
    slots[:, 0:TOK], slots[:, TOK : 2 * TOK] = slot_rows(info[1], own_ids, other)
    tokens = jnp.concatenate([own[...], other[:HALF, :]], axis=1)
    place = lax.broadcasted_iota(jnp.int32, (EXPERT_BLOCK, PAIR_ROWS, 2 * TOK), 1).astype(f32)
    for n in range(EXPERTS // EXPERT_BLOCK):
        block = slots[n * EXPERT_BLOCK : (n + 1) * EXPERT_BLOCK, :]
        hit = block[:, None, :] == place
        pick = jnp.where(hit, 1.0, 0.0).reshape(ROW_BLOCK, 2 * TOK).astype(bf16)
        rows = lax.dot_general(pick, tokens, NT, preferred_element_type=f32).astype(bf16)
        out[n * ROW_BLOCK : (n + 1) * ROW_BLOCK, :] = widened(rows)


def mixing_kernel(info, own_ids, other, own_share, out):
    own_slot, other_slot = slot_rows(info[1], own_ids, other)
    slot = jnp.concatenate([own_slot, other_slot], axis=1).T.astype(bf16)
    parts = jnp.concatenate([own_share[...], other[HALF + 16 :, :]], axis=1).astype(f32)
    high = parts[:EXPERTS].T.astype(bf16)
    rest = parts[EXPERTS:].T.astype(bf16)
    expert = lax.broadcasted_iota(jnp.int32, (EXPERTS, ROWS), 0) * PAIR_ROWS
    offset = lax.broadcasted_iota(jnp.int32, (EXPERTS, ROWS), 1) - expert
    inside = (offset >= 0) & (offset < PAIR_ROWS)
    spread = jnp.where(inside, 1.0, 0.0).astype(bf16)
    place = jnp.sum(jnp.where(inside, offset.astype(f32), 0.0), axis=0, keepdims=True)
    hit = jnp.dot(slot, spread, preferred_element_type=f32) == place
    for part, factor in enumerate((high, rest)):
        wide = jnp.dot(factor, spread, preferred_element_type=f32)
        out[part * 2 * TOK : (part + 1) * 2 * TOK, :] = jnp.where(hit, wide, 0.0).astype(bf16)


def active_kernel(info, own, other, gate_w, up_w, out):
    core = info[1]
    own_rows = pl.ds(pl.multiple_of(core * HALF, 32), HALF)
    other_rows = pl.ds(pl.multiple_of((1 - core) * HALF, 32), HALF)
    x_own = own[:, :HALF]
    x_other = other[:, :HALF]
    gate = jnp.dot(x_own, gate_w[own_rows, :], preferred_element_type=f32)
    gate += jnp.dot(x_other, gate_w[other_rows, :], preferred_element_type=f32)
    up = jnp.dot(x_own, up_w[own_rows, :], preferred_element_type=f32)
    up += jnp.dot(x_other, up_w[other_rows, :], preferred_element_type=f32)
    out[...] = (gate * jax.nn.sigmoid(swiglu_alpha * gate) * (up + 1.0)).astype(bf16)


def down_kernel(starts, info, *refs):
    count = len(starts)
    own, other = refs[:count], refs[count : 2 * count]
    down_w, other_w = refs[2 * count : 2 * count + 2]
    out = refs[-1]
    for n, start in enumerate(starts):
        first = lax.dot_general(own[n][...], down_w[...], NT, preferred_element_type=f32)
        second = lax.dot_general(other[n][...], other_w[...], NT, preferred_element_type=f32)
        both = first.astype(bf16).astype(f32) + second.astype(bf16).astype(f32)
        out[start : start + own[n].shape[0], :] = widened(both.astype(bf16))


MIX_BLOCK = 512


def mix_kernel(factors, rows, own_out, send_out):
    both = jnp.dot(factors[...], rows[...], preferred_element_type=f32)
    total = both[: 2 * TOK] + both[2 * TOK :]
    own_out[...] = total[:TOK].T
    send_out[...] = total[TOK:].T


def final_kernel(info, residual, own, other, out):
    core = info[1]
    for half, ref in ((core, own), (1 - core, other)):
        for lo in range(0, HALF, PART):
            rows = pl.ds(pl.multiple_of(half * HALF + lo, 32), PART)
            mix = ref[lo : lo + PART, :]
            out[rows, :] = (residual[rows, :].astype(f32) + mix).astype(bf16)


def params(mib):
    return pltpu.CompilerParams(vmem_limit_bytes=mib << 20)


def kernel_call(body, outs, operands, with_info=True, scratch=(), mib=40, flops=0, moved=0, remain=()):
    single = not isinstance(outs, list)
    specs = [SMEM_SPEC] * int(with_info) + [VMEM_SPEC] * (len(operands) - int(with_info))
    for n in remain:
        specs[n] = ANY_SPEC
    return pl.pallas_call(
        body,
        out_shape=outs,
        in_specs=specs,
        out_specs=VMEM_SPEC if single else [VMEM_SPEC] * len(outs),
        scratch_shapes=list(scratch),
        compiler_params=params(mib),
        cost_estimate=pl.CostEstimate(flops=flops, bytes_accessed=moved, transcendentals=0),
    )(*operands)


def shape(*dims, dtype=bf16):
    return jax.ShapeDtypeStruct(dims, dtype)


def local(
    hidden_in,
    queries,
    key_heads,
    values,
    doc_lengths,
    out_weight,
    norm_gain,
    router_weight,
    expert_ids,
    gate_weight,
    up_weight,
    down_weight,
):
    upper = lax.axis_index("xh")
    core = lax.axis_index("c")
    depth = lax.axis_index("z")
    info = jnp.stack([upper, core, doc_lengths[0], depth]).astype(jnp.int32)
    swap = [(0, 1), (1, 0)]

    own_w = out_weight.T
    half_w = lax.dynamic_slice_in_dim(own_w, core * HALF, HALF, axis=0)
    q, half_w = lax.optimization_barrier((queries[0], half_w))
    prepared = kernel_call(
        prepare_kernel, shape(4, TOK, 1280), (q, key_heads[0], values[0]), with_info=False
    )
    first_w = lax.ppermute(half_w, ("xh", "xl"), [(0, 3), (3, 0), (1, 2), (2, 1)])
    qkv = lax.all_to_all(prepared, "z", split_axis=0, concat_axis=0, tiled=True).reshape(512, 1280)
    lower = lax.ppermute(qkv[:, 1024:], "xh", [(0, 1)])
    ids = expert_ids[0].T

    def attend(a, qkv):
        return kernel_call(
            functools.partial(attention_kernel, a),
            shape(512, 512),
            (info, qkv, lower),
            scratch=(pltpu.VMEM((2, 1024, 256), bf16),) * 2 + (pltpu.VMEM((512, 256), bf16), DMA(())),
            remain=(2,),
            flops=1000,
            mib=16,
        )

    first_att = attend(0, qkv)
    first_w, first_att, qkv = lax.optimization_barrier((first_w, first_att, qkv))
    second_w = lax.ppermute(first_w, "c", swap)
    second_att = attend(1, qkv)

    plus = [(i, (i + 1) % 4) for i in range(4)]
    minus = [(i, (i + 3) % 4) for i in range(4)]
    weights = (own_w, first_w, second_w)
    half_shape = shape(HALF, TOK)
    half_float = shape(HALF, TOK, dtype=f32)
    far_low, far_high = kernel_call(
        far_kernel,
        [half_shape] * 2,
        (info, first_att, second_att) + weights,
        flops=10**9,
        mib=12,
    )

    far_low = lax.ppermute(far_low, "z", plus)
    far_high = lax.ppermute(far_high, "z", minus)
    up_low, up_high, down_low, down_high, own_part = kernel_call(
        near_kernel,
        [half_float, half_shape, half_shape, half_float, shape(D, TOK, dtype=f32)],
        (info, first_att, second_att) + weights,
        flops=2 * 10**10,
        mib=16,
    )
    high_a = lax.ppermute(up_high, "z", plus)
    low_b = lax.ppermute(down_low, "z", minus)
    relayed = (up_low + far_low.astype(f32)).astype(bf16)
    low_a = lax.ppermute(relayed, "z", plus)
    relayed_high = (down_high + far_high.astype(f32)).astype(bf16)
    high_b = lax.ppermute(relayed_high, "z", minus)

    gate_v, up_v, down_v, send_down = pl.pallas_call(
        stage_kernel,
        out_shape=[pltpu.VMEM((D, FF), bf16)] * 2 + [pltpu.VMEM((HALF, FF), bf16)] * 2,
        in_specs=[SMEM_SPEC] + [HBM_SPEC] * 3 + [ANY_SPEC],
        out_specs=[VMEM_SPEC] * 4,
        scratch_shapes=[DMA((4,))],
        compiler_params=params(16),
    )(info, gate_weight[0], up_weight[0], down_weight[0].T, relayed)
    other_down = lax.ppermute(send_down, "c", swap)
    gain = jnp.broadcast_to(norm_gain[:, None], (D, TOK))
    gain, gate_v, up_v, down_v = lax.optimization_barrier((gain, gate_v, up_v, down_v))
    residual, own_half, send_half, share = kernel_call(
        norm_kernel,
        [shape(D, TOK), half_shape, shape(HALF + 16 + 2 * EXPERTS, TOK), shape(2 * EXPERTS, TOK)],
        (info, own_part, low_a, low_b, high_a, high_b, hidden_in[0].T, gain, router_weight.T, ids),
        scratch=(pltpu.VMEM((D, TOK), bf16), pltpu.VMEM((4, HALF, TOK), bf16), DMA((4,))),
        remain=(2, 3, 4, 5),
        mib=12,
    )
    other_half = lax.ppermute(send_half, "c", swap)

    outgoing = kernel_call(
        dispatch_kernel,
        shape(ROWS, WIDE),
        (info, own_half, other_half, ids),
        scratch=(pltpu.VMEM((EXPERTS, 2 * TOK), f32),),
        mib=16,
    )
    chips = ("z", "xh", "xl", "y")

    def across(rows):
        return lax.all_to_all(
            rows.reshape(EXPERTS, PAIR_ROWS, WIDE), chips, split_axis=0, concat_axis=0, tiled=True
        ).reshape(ROWS, WIDE)

    arrived = across(outgoing)
    arrived, share = lax.optimization_barrier((arrived, share))
    factors = kernel_call(
        mixing_kernel,
        shape(4 * TOK, ROWS),
        (info, ids, other_half, share),
        mib=16,
    )
    own_active, other_active = [], []
    for start, count in STEPS:
        rows = arrived[start : start + count]
        if len(own_active) == 1:
            rows, rows_other = lax.optimization_barrier((rows, rows_other))
        elif own_active:
            rows, rows_other, own_active[0] = lax.optimization_barrier(
                (rows, rows_other, own_active[0])
            )
        rows_other = lax.ppermute(rows, "c", swap)
        if not own_active:
            rows_other, factors = lax.optimization_barrier((rows_other, factors))
        if len(own_active) == 2:
            rows_other, other_active[0] = lax.optimization_barrier((rows_other, other_active[0]))
        active = kernel_call(
            active_kernel,
            shape(count, FF),
            (info, rows, rows_other, gate_v, up_v),
            flops=45 * 10**8,
            mib=20,
        )
        own_active.append(active)
        other_active.append(lax.ppermute(active, "c", swap))

    def down(steps, *buffer):
        picked = [own_active[n] for n in steps] + [other_active[n] for n in steps]
        operands = (info, *picked, down_v, other_down, *buffer)
        return pl.pallas_call(
            functools.partial(down_kernel, [STEPS[n][0] for n in steps]),
            out_shape=shape(ROWS, WIDE),
            in_specs=[SMEM_SPEC] + [VMEM_SPEC] * (len(operands) - 1),
            out_specs=VMEM_SPEC,
            input_output_aliases={len(operands) - 1: 0} if buffer else {},
            compiler_params=params(24),
        )(*operands)

    expert_out = down([2], down([0, 1]))
    own_mix, send_mix = pl.pallas_call(
        mix_kernel,
        grid=(WIDE // MIX_BLOCK,),
        out_shape=[shape(WIDE, TOK, dtype=f32)] * 2,
        in_specs=[
            pl.BlockSpec((4 * TOK, ROWS), lambda i: (0, 0)),
            pl.BlockSpec((ROWS, MIX_BLOCK), lambda i: (0, i)),
        ],
        out_specs=[pl.BlockSpec((MIX_BLOCK, TOK), lambda i: (i, 0))] * 2,
        compiler_params=params(32),
    )(factors, across(expert_out))
    other_mix = lax.ppermute(send_mix, "c", swap)
    layer_out = kernel_call(
        final_kernel, shape(D, TOK), (info, residual, own_mix, other_mix), mib=12
    )
    return layer_out.T[None]


def solution(mesh):
    split_mesh = Mesh(mesh.devices.reshape(2, 4, 2, 4, 2), ("xh", "z", "xl", "y", "c"))
    seq = ("xh", "z")
    doc = ("xl", "y", "c")
    in_specs = (
        P(doc, seq, None),
        P(doc, seq, None),
        P(doc, seq, None),
        P(doc, seq, None),
        P(doc),
        P(seq, None),
        P(),
        P(),
        P(doc, seq, None),
        P(seq + doc, None, None),
        P(seq + doc, None, None),
        P(seq + doc, None, None),
    )
    return jax.shard_map(
        local,
        mesh=split_mesh,
        in_specs=in_specs,
        out_specs=P(doc, seq, None),
        check_vma=False,
    )
```

```python
import functools
import jax
import jax.numpy as jnp
from jax import lax
from jax.experimental import pallas as pl
from jax.experimental.pallas import tpu as pltpu
from jax.sharding import Mesh, PartitionSpec as P

HD = 64
TOP = 4
EXPERTS = 64
TOK = 128
D = 2880
FF = 768
HALF = D // 2
WIDE = 1536
CAP = 12
PAIR_ROWS = 2 * CAP
ROWS = EXPERTS * PAIR_ROWS
PART = 480
STEPS = ((0, 256), (256, 640), (896, 640))

negative_fill = -1e30
swiglu_alpha = 1.702
norm_eps = 1e-05
exp_scale = HD ** (-0.5) * 1.4426950408889634

f32 = jnp.float32
bf16 = jnp.bfloat16
VMEM_SPEC = pl.BlockSpec(memory_space=pltpu.VMEM)
SMEM_SPEC = pl.BlockSpec(memory_space=pltpu.SMEM)
HBM_SPEC = pl.BlockSpec(memory_space=pltpu.HBM)
ANY_SPEC = pl.BlockSpec(memory_space=pl.ANY)
DMA = pltpu.SemaphoreType.DMA
NT = (((1,), (1,)), ((), ()))


def prepare_kernel(queries, key_heads, values, out):
    lane = lax.broadcasted_iota(jnp.int32, (TOK, 128), 1)
    for z in range(4):
        out[z, :, 0:512] = queries[:, z * 512 : z * 512 + 512]
        out[z, :, 512:1024] = queries[:, 2048 + z * 512 : 2560 + z * 512]
        tile = (z // 2) * 128
        for n, ref in enumerate((key_heads, values)):
            first = ref[:, tile : tile + 128].astype(f32)
            second = ref[:, 256 + tile : 384 + tile].astype(f32)
            if z % 2 == 0:
                second = pltpu.roll(second, 64, 1)
            else:
                first = pltpu.roll(first, 64, 1)
            out[z, :, 1024 + 128 * n : 1152 + 128 * n] = jnp.where(
                lane < 64, first, second
            ).astype(bf16)


def attention_kernel(a, info, qkv, lower_ref, att, keys, vals, lower, sem):
    upper = info[0]
    doc_len = info[2]
    fetch = pltpu.make_async_copy(lower_ref, lower, sem)
    fetch.start()
    fetch.wait()
    lane = lax.broadcasted_iota(jnp.int32, (512, 128), 1)
    low = lane < 64
    one = jnp.ones((512, 128), f32)
    row = lax.broadcasted_iota(jnp.int32, (512, 128), 0)
    for side in range(2):
        rows = pl.ds(512 * side, 512)
        source = qkv[:, 1024:1280] if side else lower[...]
        kk = source[:, 0:128].astype(f32)
        vv = source[:, 128:256].astype(f32)
        kr = pltpu.roll(kk, 64, 1)
        vr = pltpu.roll(vv, 64, 1)
        position = row + 512 * upper if side else row
        masked = (lane == 0) & (position >= doc_len)
        bias = jnp.where(masked, negative_fill, 0.0).astype(bf16)
        for par in range(2):
            keep = low if par == 0 else ~low
            keys[par, rows, 0:128] = jnp.where(keep, kk if a == par else kr, 0.0).astype(bf16)
            keys[par, rows, 128:256] = bias
            vals[par, rows, 0:128] = jnp.where(keep, vv if a == par else vr, 0.0).astype(bf16)
            vals[par, rows, 128:256] = jnp.where(keep, one, 0.0).astype(bf16)

    first_lane = jnp.where(lane == 0, 1.0, 0.0).astype(bf16)
    causal = jnp.where(
        lax.broadcasted_iota(jnp.int32, (128, 128), 1)
        <= lax.broadcasted_iota(jnp.int32, (128, 128), 0),
        0.0,
        negative_fill,
    )
    causal = jnp.concatenate([causal] * 4, axis=0)

    def block(i, with_other):
        nk = (i + 1) * 128 + (512 if with_other else 0)
        start = 0 if with_other else 512
        q_rows = slice(i * 128, (i + 1) * 128)
        q_tiles = [qkv[q_rows, a * 512 + 128 * t : a * 512 + 128 * (t + 1)] for t in range(4)]
        q_stack = jnp.concatenate([jnp.concatenate(q_tiles, axis=0), first_lane], axis=1)
        total = None
        for par in range(2):
            k_blk = keys[par, start : start + nk, :]
            scores = lax.dot_general(q_stack, k_blk, NT, preferred_element_type=f32)
            last = scores[:, nk - 128 :] + causal
            if nk > 128:
                scores = jnp.concatenate([scores[:, : nk - 128], last], axis=1)
            else:
                scores = last
            top = jnp.max(scores, axis=1, keepdims=True)
            weights = jnp.exp2((scores - top) * exp_scale).astype(bf16)
            part = jnp.dot(
                weights, vals[par, start : start + nk, :], preferred_element_type=f32
            )
            total = part if total is None else total + part
        result = (total[:, 0:128] / total[:, 128:256]).astype(bf16)
        for t in range(4):
            att[q_rows, 128 * t : 128 * (t + 1)] = result[128 * t : 128 * (t + 1)]

    @pl.when(upper == 1)
    def _():
        for i in range(4):
            block(i, True)

    @pl.when(upper == 0)
    def _():
        for i in range(4):
            block(i, False)


def pick_attended(upper, first_att, second_att, rows):
    first, second = first_att[rows, :], second_att[rows, :]
    return jnp.where(upper == 0, first, second), jnp.where(upper == 0, second, first)


def project(core, own, other, own_w, first_w, second_w, store):
    for half in range(2):
        for lo in range(0, HALF, PART):
            rows = slice(half * HALF + lo, half * HALF + lo + PART)
            far = slice(lo, lo + PART)
            far_w = jnp.where(core == half, first_w[far, :], second_w[far, :])
            term = lax.dot_general(own_w[rows, :], own, NT, preferred_element_type=f32)
            term += lax.dot_general(far_w, other, NT, preferred_element_type=f32)
            store(half, far, term)


def token_block(z, shift):
    return pl.ds(pl.multiple_of(lax.rem(z + shift, 4) * TOK, TOK), TOK)


def far_kernel(info, first_att, second_att, own_w, first_w, second_w, low_out, high_out):
    own, other = pick_attended(info[0], first_att, second_att, token_block(info[3], 2))

    def store(half, rows, term):
        (low_out, high_out)[half][rows, :] = term.astype(bf16)

    project(info[1], own, other, own_w, first_w, second_w, store)


def near_kernel(
    info, first_att, second_att, own_w, first_w, second_w, up_low, up_high, down_low, down_high, own_out
):
    picked = [
        pick_attended(info[0], first_att, second_att, token_block(info[3], shift))
        for shift in (1, 3, 0)
    ]
    own = jnp.concatenate([p[0] for p in picked], axis=0)
    other = jnp.concatenate([p[1] for p in picked], axis=0)

    def store(half, rows, term):
        up, down = ((up_low, down_low), (up_high, down_high))[half]
        up[rows, :] = term[:, :TOK].astype(up.dtype)
        down[rows, :] = term[:, TOK : 2 * TOK].astype(down.dtype)
        own_out[slice(half * HALF + rows.start, half * HALF + rows.stop), :] = term[:, 2 * TOK :]

    project(info[1], own, other, own_w, first_w, second_w, store)


def stage_kernel(info, gate_w, up_w, down_w, ready, gate_out, up_out, down_out, send_out, sems):
    own_rows = pl.ds(pl.multiple_of(info[1] * HALF, 32), HALF)
    other_rows = pl.ds(pl.multiple_of((1 - info[1]) * HALF, 32), HALF)
    copies = [
        pltpu.make_async_copy(down_w.at[other_rows, :], send_out, sems.at[3]),
        pltpu.make_async_copy(gate_w, gate_out, sems.at[0]),
        pltpu.make_async_copy(up_w, up_out, sems.at[1]),
        pltpu.make_async_copy(down_w.at[own_rows, :], down_out, sems.at[2]),
    ]
    for copy in copies:
        copy.start()
    for copy in copies:
        copy.wait()


def presum_kernel(own_part, low, high, hidden, out):
    for half, ref in enumerate((low, high)):
        for lo in range(0, HALF, PART):
            rows = slice(half * HALF + lo, half * HALF + lo + PART)
            acc = hidden[rows, :].astype(f32) + own_part[rows, :]
            out[rows, :] = acc + ref[lo : lo + PART, :].astype(f32)


def norm_kernel(
    info, base, low, high, gain, router, ids, residual_out, own_out, send_out, share_out, normed, held, sems
):
    core = info[1]
    copies = [
        pltpu.make_async_copy(ref, held.at[n], sems.at[n]) for n, ref in enumerate((low, high))
    ]
    for copy in copies:
        copy.start()
    for copy in copies:
        copy.wait()
    square = jnp.zeros((1, TOK), f32)
    for half in range(2):
        for lo in range(0, HALF, PART):
            rows = slice(half * HALF + lo, half * HALF + lo + PART)
            acc = base[rows, :] + held[half, lo : lo + PART, :].astype(f32)
            rounded = acc.astype(bf16)
            residual_out[rows, :] = rounded
            res = rounded.astype(f32)
            square = square + jnp.sum(res * res, axis=0, keepdims=True)
    factor = lax.rsqrt(square * (1.0 / D) + norm_eps)
    for lo in range(0, D, PART):
        rows = slice(lo, lo + PART)
        res = residual_out[rows, :].astype(f32)
        normed[rows, :] = (res * factor * gain[rows, :].astype(f32)).astype(bf16)
    logits = jnp.dot(router[...], normed[...], preferred_element_type=f32)
    logits = jnp.concatenate(
        [logits[(xh * 4 + z) * 8 : (xh * 4 + z) * 8 + 8] for z in range(4) for xh in range(2)], axis=0
    )
    named = named_of(ids[...])
    raised = jnp.where(named, jnp.exp(logits), 0.0)
    share = raised / jnp.sum(raised, axis=0, keepdims=True)
    high = share.astype(bf16)
    share_out[:EXPERTS, :] = high
    share_out[EXPERTS:, :] = (share - high.astype(f32)).astype(bf16)
    own_out[...] = normed[pl.ds(pl.multiple_of(core * HALF, 32), HALF), :]
    send_out[:HALF, :] = normed[pl.ds(pl.multiple_of((1 - core) * HALF, 32), HALF), :]
    send_out[HALF + 16 :, :] = share_out[...]
    send_out[HALF : HALF + 16, :] = jnp.concatenate(
        [ids[...].astype(f32), jnp.zeros((16 - TOP, TOK), f32)], axis=0
    ).astype(bf16)


def named_of(ids):
    place = lax.broadcasted_iota(jnp.int32, (EXPERTS, TOK), 0)
    expert = ((place >> 3) & 1) * 32 + (place >> 4) * 8 + (place & 7)
    named = expert == ids[0:1, :]
    for k in range(1, TOP):
        named = named | (expert == ids[k : k + 1, :])
    return named


def slots_of(ids, offset):
    named = named_of(ids)
    before = lax.broadcasted_iota(jnp.int32, (TOK, TOK), 0) < lax.broadcasted_iota(
        jnp.int32, (TOK, TOK), 1
    )
    rank = jnp.dot(
        named.astype(f32).astype(bf16), before.astype(f32).astype(bf16), preferred_element_type=f32
    )
    return jnp.where(named, rank + offset, -1.0)


def slot_rows(core, own_ids, other):
    start = (core * CAP).astype(f32)
    other_ids = other[HALF : HALF + 16, :].astype(f32).astype(jnp.int32)
    return slots_of(own_ids[...], start), slots_of(other_ids, CAP - start)


def widened(rows):
    return jnp.concatenate([rows, jnp.zeros((rows.shape[0], WIDE - HALF), rows.dtype)], axis=1)


EXPERT_BLOCK = 16
ROW_BLOCK = EXPERT_BLOCK * PAIR_ROWS


def dispatch_kernel(info, own, other, own_ids, out, slots):
    slots[:, 0:TOK], slots[:, TOK : 2 * TOK] = slot_rows(info[1], own_ids, other)
    tokens = jnp.concatenate([own[...], other[:HALF, :]], axis=1)
    place = lax.broadcasted_iota(jnp.int32, (EXPERT_BLOCK, PAIR_ROWS, 2 * TOK), 1).astype(f32)
    for n in range(EXPERTS // EXPERT_BLOCK):
        block = slots[n * EXPERT_BLOCK : (n + 1) * EXPERT_BLOCK, :]
        hit = block[:, None, :] == place
        pick = jnp.where(hit, 1.0, 0.0).reshape(ROW_BLOCK, 2 * TOK).astype(bf16)
        rows = lax.dot_general(pick, tokens, NT, preferred_element_type=f32).astype(bf16)
        out[n * ROW_BLOCK : (n + 1) * ROW_BLOCK, :] = widened(rows)


def mixing_kernel(info, own_ids, other, own_share, out):
    own_slot, other_slot = slot_rows(info[1], own_ids, other)
    slot = jnp.concatenate([own_slot, other_slot], axis=1).T.astype(bf16)
    parts = jnp.concatenate([own_share[...], other[HALF + 16 :, :]], axis=1).astype(f32)
    high = parts[:EXPERTS].T.astype(bf16)
    rest = parts[EXPERTS:].T.astype(bf16)
    expert = lax.broadcasted_iota(jnp.int32, (EXPERTS, ROWS), 0) * PAIR_ROWS
    offset = lax.broadcasted_iota(jnp.int32, (EXPERTS, ROWS), 1) - expert
    inside = (offset >= 0) & (offset < PAIR_ROWS)
    spread = jnp.where(inside, 1.0, 0.0).astype(bf16)
    place = jnp.sum(jnp.where(inside, offset.astype(f32), 0.0), axis=0, keepdims=True)
    hit = jnp.dot(slot, spread, preferred_element_type=f32) == place
    for part, factor in enumerate((high, rest)):
        wide = jnp.dot(factor, spread, preferred_element_type=f32)
        out[part * 2 * TOK : (part + 1) * 2 * TOK, :] = jnp.where(hit, wide, 0.0).astype(bf16)


def active_kernel(info, own, other, gate_w, up_w, out):
    core = info[1]
    own_rows = pl.ds(pl.multiple_of(core * HALF, 32), HALF)
    other_rows = pl.ds(pl.multiple_of((1 - core) * HALF, 32), HALF)
    x_own = own[:, :HALF]
    x_other = other[:, :HALF]
    gate = jnp.dot(x_own, gate_w[own_rows, :], preferred_element_type=f32)
    gate += jnp.dot(x_other, gate_w[other_rows, :], preferred_element_type=f32)
    up = jnp.dot(x_own, up_w[own_rows, :], preferred_element_type=f32)
    up += jnp.dot(x_other, up_w[other_rows, :], preferred_element_type=f32)
    out[...] = (gate * jax.nn.sigmoid(swiglu_alpha * gate) * (up + 1.0)).astype(bf16)


def down_kernel(starts, info, *refs):
    count = len(starts)
    own, other = refs[:count], refs[count : 2 * count]
    down_w, other_w = refs[2 * count : 2 * count + 2]
    out = refs[-1]
    for n, start in enumerate(starts):
        first = lax.dot_general(own[n][...], down_w[...], NT, preferred_element_type=f32)
        second = lax.dot_general(other[n][...], other_w[...], NT, preferred_element_type=f32)
        both = first.astype(bf16).astype(f32) + second.astype(bf16).astype(f32)
        out[start : start + own[n].shape[0], :] = widened(both.astype(bf16))


MIX_BLOCK = 512


def mix_kernel(factors, rows, own_out, send_out):
    for lo in range(0, WIDE, MIX_BLOCK):
        columns = slice(lo, lo + MIX_BLOCK)
        both = jnp.dot(factors[...], rows[:, columns], preferred_element_type=f32)
        total = both[: 2 * TOK] + both[2 * TOK :]
        own_out[columns, :] = total[:TOK].T
        send_out[columns, :] = total[TOK:].T.astype(bf16)


def final_kernel(info, residual, own, other, out):
    core = info[1]
    for half, ref in ((core, own), (1 - core, other)):
        for lo in range(0, HALF, PART):
            rows = pl.ds(pl.multiple_of(half * HALF + lo, 32), PART)
            mix = ref[lo : lo + PART, :].astype(f32)
            out[rows, :] = (residual[rows, :].astype(f32) + mix).astype(bf16)


def params(mib):
    return pltpu.CompilerParams(vmem_limit_bytes=mib << 20)


def kernel_call(body, outs, operands, with_info=True, scratch=(), mib=40, flops=0, moved=0, remain=()):
    single = not isinstance(outs, list)
    specs = [SMEM_SPEC] * int(with_info) + [VMEM_SPEC] * (len(operands) - int(with_info))
    for n in remain:
        specs[n] = ANY_SPEC
    return pl.pallas_call(
        body,
        out_shape=outs,
        in_specs=specs,
        out_specs=VMEM_SPEC if single else [VMEM_SPEC] * len(outs),
        scratch_shapes=list(scratch),
        compiler_params=params(mib),
        cost_estimate=pl.CostEstimate(flops=flops, bytes_accessed=moved, transcendentals=0),
    )(*operands)


def shape(*dims, dtype=bf16):
    return jax.ShapeDtypeStruct(dims, dtype)


def local(
    hidden_in,
    queries,
    key_heads,
    values,
    doc_lengths,
    out_weight,
    norm_gain,
    router_weight,
    expert_ids,
    gate_weight,
    up_weight,
    down_weight,
):
    upper = lax.axis_index("xh")
    core = lax.axis_index("c")
    depth = lax.axis_index("z")
    info = jnp.stack([upper, core, doc_lengths[0], depth]).astype(jnp.int32)
    swap = [(0, 1), (1, 0)]

    own_w = out_weight.T
    half_w = lax.dynamic_slice_in_dim(own_w, core * HALF, HALF, axis=0)
    q, half_w = lax.optimization_barrier((queries[0], half_w))
    prepared = kernel_call(
        prepare_kernel, shape(4, TOK, 1280), (q, key_heads[0], values[0]), with_info=False
    )
    first_w = lax.ppermute(half_w, ("xh", "xl"), [(0, 3), (3, 0), (1, 2), (2, 1)])
    qkv = lax.all_to_all(prepared, "z", split_axis=0, concat_axis=0, tiled=True).reshape(512, 1280)
    lower = lax.ppermute(qkv[:, 1024:], "xh", [(0, 1)])
    ids = expert_ids[0].T

    def attend(a, qkv):
        return kernel_call(
            functools.partial(attention_kernel, a),
            shape(512, 512),
            (info, qkv, lower),
            scratch=(pltpu.VMEM((2, 1024, 256), bf16),) * 2 + (pltpu.VMEM((512, 256), bf16), DMA(())),
            remain=(2,),
            flops=1000,
            mib=16,
        )

    first_att = attend(0, qkv)
    first_w, first_att, qkv = lax.optimization_barrier((first_w, first_att, qkv))
    second_w = lax.ppermute(first_w, "c", swap)
    second_att = attend(1, qkv)

    plus = [(i, (i + 1) % 4) for i in range(4)]
    minus = [(i, (i + 3) % 4) for i in range(4)]
    weights = (own_w, first_w, second_w)
    half_shape = shape(HALF, TOK)
    half_float = shape(HALF, TOK, dtype=f32)
    far_low, far_high = kernel_call(
        far_kernel,
        [half_shape] * 2,
        (info, first_att, second_att) + weights,
        flops=10**9,
        mib=12,
    )

    far_low = lax.ppermute(far_low, "z", plus)
    far_high = lax.ppermute(far_high, "z", minus)
    up_low, up_high, down_low, down_high, own_part = kernel_call(
        near_kernel,
        [half_float, half_shape, half_shape, half_float, shape(D, TOK, dtype=f32)],
        (info, first_att, second_att) + weights,
        flops=2 * 10**10,
        mib=16,
    )
    high_a = lax.ppermute(up_high, "z", plus)
    low_b = lax.ppermute(down_low, "z", minus)
    relayed = (up_low + far_low.astype(f32)).astype(bf16)
    low_a = lax.ppermute(relayed, "z", plus)
    relayed_high = (down_high + far_high.astype(f32)).astype(bf16)
    high_b = lax.ppermute(relayed_high, "z", minus)

    gate_v, up_v, down_v, send_down = pl.pallas_call(
        stage_kernel,
        out_shape=[pltpu.VMEM((D, FF), bf16)] * 2 + [pltpu.VMEM((HALF, FF), bf16)] * 2,
        in_specs=[SMEM_SPEC] + [HBM_SPEC] * 3 + [ANY_SPEC],
        out_specs=[VMEM_SPEC] * 4,
        scratch_shapes=[DMA((4,))],
        compiler_params=params(16),
    )(info, gate_weight[0], up_weight[0], down_weight[0].T, relayed)
    other_down = lax.ppermute(send_down, "c", swap)
    gain = jnp.broadcast_to(norm_gain[:, None], (D, TOK))
    base = kernel_call(
        presum_kernel,
        shape(D, TOK, dtype=f32),
        (own_part, low_b, high_a, hidden_in[0].T),
        with_info=False,
        mib=12,
    )
    gain, gate_v, up_v, down_v = lax.optimization_barrier((gain, gate_v, up_v, down_v))
    residual, own_half, send_half, share = kernel_call(
        norm_kernel,
        [shape(D, TOK), half_shape, shape(HALF + 16 + 2 * EXPERTS, TOK), shape(2 * EXPERTS, TOK)],
        (info, base, low_a, high_b, gain, router_weight.T, ids),
        scratch=(pltpu.VMEM((D, TOK), bf16), pltpu.VMEM((2, HALF, TOK), bf16), DMA((2,))),
        remain=(2, 3),
        mib=12,
    )
    other_half = lax.ppermute(send_half, "c", swap)

    outgoing = kernel_call(
        dispatch_kernel,
        shape(ROWS, WIDE),
        (info, own_half, other_half, ids),
        scratch=(pltpu.VMEM((EXPERTS, 2 * TOK), f32),),
        mib=16,
    )
    chips = ("z", "xh", "xl", "y")

    def across(rows):
        return lax.all_to_all(
            rows.reshape(EXPERTS, PAIR_ROWS, WIDE), chips, split_axis=0, concat_axis=0, tiled=True
        ).reshape(ROWS, WIDE)

    arrived = across(outgoing)
    arrived, share = lax.optimization_barrier((arrived, share))
    factors = kernel_call(
        mixing_kernel,
        shape(4 * TOK, ROWS),
        (info, ids, other_half, share),
        mib=16,
    )
    own_active, other_active = [], []
    for start, count in STEPS:
        rows = arrived[start : start + count]
        if len(own_active) == 1:
            rows, rows_other = lax.optimization_barrier((rows, rows_other))
        elif own_active:
            rows, rows_other, own_active[0] = lax.optimization_barrier(
                (rows, rows_other, own_active[0])
            )
        rows_other = lax.ppermute(rows, "c", swap)
        if not own_active:
            rows_other, factors = lax.optimization_barrier((rows_other, factors))
        if len(own_active) == 2:
            rows_other, other_active[0] = lax.optimization_barrier((rows_other, other_active[0]))
        active = kernel_call(
            active_kernel,
            shape(count, FF),
            (info, rows, rows_other, gate_v, up_v),
            flops=45 * 10**8,
            mib=20,
        )
        own_active.append(active)
        other_active.append(lax.ppermute(active, "c", swap))

    def down(steps, *buffer):
        picked = [own_active[n] for n in steps] + [other_active[n] for n in steps]
        operands = (info, *picked, down_v, other_down, *buffer)
        return pl.pallas_call(
            functools.partial(down_kernel, [STEPS[n][0] for n in steps]),
            out_shape=shape(ROWS, WIDE),
            in_specs=[SMEM_SPEC] + [VMEM_SPEC] * (len(operands) - 1),
            out_specs=VMEM_SPEC,
            input_output_aliases={len(operands) - 1: 0} if buffer else {},
            compiler_params=params(24),
        )(*operands)

    expert_out = down([2], down([0, 1]))
    own_mix, send_mix = kernel_call(
        mix_kernel,
        [shape(WIDE, TOK, dtype=f32), shape(WIDE, TOK)],
        (factors, across(expert_out)),
        with_info=False,
        mib=24,
    )
    other_mix = lax.ppermute(send_mix, "c", swap)
    layer_out = kernel_call(
        final_kernel, shape(D, TOK), (info, residual, own_mix, other_mix), mib=12
    )
    return layer_out.T[None]


def solution(mesh):
    split_mesh = Mesh(mesh.devices.reshape(2, 4, 2, 4, 2), ("xh", "z", "xl", "y", "c"))
    seq = ("xh", "z")
    doc = ("xl", "y", "c")
    in_specs = (
        P(doc, seq, None),
        P(doc, seq, None),
        P(doc, seq, None),
        P(doc, seq, None),
        P(doc),
        P(seq, None),
        P(),
        P(),
        P(doc, seq, None),
        P(seq + doc, None, None),
        P(seq + doc, None, None),
        P(seq + doc, None, None),
    )
    return jax.shard_map(
        local,
        mesh=split_mesh,
        in_specs=in_specs,
        out_specs=P(doc, seq, None),
        check_vma=False,
    )
```

```python
import functools
import jax
import jax.numpy as jnp
from jax import lax
from jax.experimental import pallas as pl
from jax.experimental.pallas import tpu as pltpu
from jax.sharding import Mesh, PartitionSpec as P

HD = 64
TOP = 4
EXPERTS = 64
TOK = 128
D = 2880
FF = 768
HALF = D // 2
WIDE = 1536
CAP = 12
PAIR_ROWS = 2 * CAP
ROWS = EXPERTS * PAIR_ROWS
PART = 480
STEPS = ((0, 256), (256, 640), (896, 640))

negative_fill = -1e30
swiglu_alpha = 1.702
norm_eps = 1e-05
exp_scale = HD ** (-0.5) * 1.4426950408889634

f32 = jnp.float32
bf16 = jnp.bfloat16
VMEM_SPEC = pl.BlockSpec(memory_space=pltpu.VMEM)
SMEM_SPEC = pl.BlockSpec(memory_space=pltpu.SMEM)
HBM_SPEC = pl.BlockSpec(memory_space=pltpu.HBM)
ANY_SPEC = pl.BlockSpec(memory_space=pl.ANY)
DMA = pltpu.SemaphoreType.DMA
NT = (((1,), (1,)), ((), ()))


def prepare_kernel(queries, key_heads, values, out):
    lane = lax.broadcasted_iota(jnp.int32, (TOK, 128), 1)
    for z in range(4):
        out[z, :, 0:512] = queries[:, z * 512 : z * 512 + 512]
        out[z, :, 512:1024] = queries[:, 2048 + z * 512 : 2560 + z * 512]
        tile = (z // 2) * 128
        for n, ref in enumerate((key_heads, values)):
            first = ref[:, tile : tile + 128].astype(f32)
            second = ref[:, 256 + tile : 384 + tile].astype(f32)
            if z % 2 == 0:
                second = pltpu.roll(second, 64, 1)
            else:
                first = pltpu.roll(first, 64, 1)
            out[z, :, 1024 + 128 * n : 1152 + 128 * n] = jnp.where(
                lane < 64, first, second
            ).astype(bf16)


def attention_kernel(a, info, qkv, lower_ref, att, keys, vals, lower, sem):
    upper = info[0]
    doc_len = info[2]
    fetch = pltpu.make_async_copy(lower_ref, lower, sem)
    fetch.start()
    fetch.wait()
    lane = lax.broadcasted_iota(jnp.int32, (512, 128), 1)
    low = lane < 64
    one = jnp.ones((512, 128), f32)
    row = lax.broadcasted_iota(jnp.int32, (512, 128), 0)
    for side in range(2):
        rows = pl.ds(512 * side, 512)
        source = qkv[:, 1024:1280] if side else lower[...]
        kk = source[:, 0:128].astype(f32)
        vv = source[:, 128:256].astype(f32)
        kr = pltpu.roll(kk, 64, 1)
        vr = pltpu.roll(vv, 64, 1)
        position = row + 512 * upper if side else row
        masked = (lane == 0) & (position >= doc_len)
        bias = jnp.where(masked, negative_fill, 0.0).astype(bf16)
        for par in range(2):
            keep = low if par == 0 else ~low
            keys[par, rows, 0:128] = jnp.where(keep, kk if a == par else kr, 0.0).astype(bf16)
            keys[par, rows, 128:256] = bias
            vals[par, rows, 0:128] = jnp.where(keep, vv if a == par else vr, 0.0).astype(bf16)
            vals[par, rows, 128:256] = jnp.where(keep, one, 0.0).astype(bf16)

    first_lane = jnp.where(lane == 0, 1.0, 0.0).astype(bf16)
    causal = jnp.where(
        lax.broadcasted_iota(jnp.int32, (128, 128), 1)
        <= lax.broadcasted_iota(jnp.int32, (128, 128), 0),
        0.0,
        negative_fill,
    )
    causal = jnp.concatenate([causal] * 4, axis=0)

    def score(i, par, with_other):
        nk = (i + 1) * 128 + (512 if with_other else 0)
        start = 0 if with_other else 512
        q_rows = slice(i * 128, (i + 1) * 128)
        q_tiles = [qkv[q_rows, a * 512 + 128 * t : a * 512 + 128 * (t + 1)] for t in range(4)]
        q_stack = jnp.concatenate([jnp.concatenate(q_tiles, axis=0), first_lane], axis=1)
        k_blk = keys[par, start : start + nk, :]
        scores = lax.dot_general(q_stack, k_blk, NT, preferred_element_type=f32)
        last = scores[:, nk - 128 :] + causal
        if nk == 128:
            return last
        return jnp.concatenate([scores[:, : nk - 128], last], axis=1)

    def attend(with_other):
        steps = [(i, par) for i in range(4) for par in range(2)]
        ahead = score(*steps[0], with_other)
        total = None
        for n, (i, par) in enumerate(steps):
            scores = ahead
            if n + 1 < len(steps):
                ahead = score(*steps[n + 1], with_other)
            start = 0 if with_other else 512
            top = jnp.max(scores, axis=1, keepdims=True)
            weights = jnp.exp2((scores - top) * exp_scale).astype(bf16)
            part = jnp.dot(
                weights,
                vals[par, start : start + scores.shape[1], :],
                preferred_element_type=f32,
            )
            if par == 0:
                total = part
                continue
            total = total + part
            result = (total[:, 0:128] / total[:, 128:256]).astype(bf16)
            for t in range(4):
                att[i * 128 : (i + 1) * 128, 128 * t : 128 * (t + 1)] = result[
                    128 * t : 128 * (t + 1)
                ]

    pl.when(upper == 1)(lambda: attend(True))
    pl.when(upper == 0)(lambda: attend(False))


def pick_attended(upper, first_att, second_att, rows):
    first, second = first_att[rows, :], second_att[rows, :]
    return jnp.where(upper == 0, first, second), jnp.where(upper == 0, second, first)


def project(core, own, other, own_w, first_w, second_w, store):
    for half in range(2):
        for lo in range(0, HALF, PART):
            rows = slice(half * HALF + lo, half * HALF + lo + PART)
            far = slice(lo, lo + PART)
            far_w = jnp.where(core == half, first_w[far, :], second_w[far, :])
            term = lax.dot_general(own_w[rows, :], own, NT, preferred_element_type=f32)
            term += lax.dot_general(far_w, other, NT, preferred_element_type=f32)
            store(half, far, term)


def token_block(z, shift):
    return pl.ds(pl.multiple_of(lax.rem(z + shift, 4) * TOK, TOK), TOK)


def far_kernel(info, first_att, second_att, own_w, first_w, second_w, low_out, high_out):
    own, other = pick_attended(info[0], first_att, second_att, token_block(info[3], 2))

    def store(half, rows, term):
        (low_out, high_out)[half][rows, :] = term.astype(bf16)

    project(info[1], own, other, own_w, first_w, second_w, store)


def near_kernel(
    info, first_att, second_att, own_w, first_w, second_w, up_low, up_high, down_low, down_high, own_out
):
    picked = [
        pick_attended(info[0], first_att, second_att, token_block(info[3], shift))
        for shift in (1, 3, 0)
    ]
    own = jnp.concatenate([p[0] for p in picked], axis=0)
    other = jnp.concatenate([p[1] for p in picked], axis=0)

    def store(half, rows, term):
        up, down = ((up_low, down_low), (up_high, down_high))[half]
        up[rows, :] = term[:, :TOK].astype(up.dtype)
        down[rows, :] = term[:, TOK : 2 * TOK].astype(down.dtype)
        own_out[slice(half * HALF + rows.start, half * HALF + rows.stop), :] = term[:, 2 * TOK :]

    project(info[1], own, other, own_w, first_w, second_w, store)


def stage_kernel(info, gate_w, up_w, down_w, ready, gate_out, up_out, down_out, send_out, sems):
    own_rows = pl.ds(pl.multiple_of(info[1] * HALF, 32), HALF)
    other_rows = pl.ds(pl.multiple_of((1 - info[1]) * HALF, 32), HALF)
    copies = [
        pltpu.make_async_copy(down_w.at[other_rows, :], send_out, sems.at[3]),
        pltpu.make_async_copy(gate_w, gate_out, sems.at[0]),
        pltpu.make_async_copy(up_w, up_out, sems.at[1]),
        pltpu.make_async_copy(down_w.at[own_rows, :], down_out, sems.at[2]),
    ]
    for copy in copies:
        copy.start()
    for copy in copies:
        copy.wait()


def presum_kernel(own_part, low, high, hidden, out):
    for half, ref in enumerate((low, high)):
        for lo in range(0, HALF, PART):
            rows = slice(half * HALF + lo, half * HALF + lo + PART)
            acc = hidden[rows, :].astype(f32) + own_part[rows, :]
            out[rows, :] = acc + ref[lo : lo + PART, :].astype(f32)


def norm_kernel(
    info, base, low, high, gain, router, ids, residual_out, own_out, send_out, share_out, normed, held, sems
):
    core = info[1]
    copies = [
        pltpu.make_async_copy(ref, held.at[n], sems.at[n]) for n, ref in enumerate((low, high))
    ]
    for copy in copies:
        copy.start()
    for copy in copies:
        copy.wait()
    square = jnp.zeros((1, TOK), f32)
    for half in range(2):
        for lo in range(0, HALF, PART):
            rows = slice(half * HALF + lo, half * HALF + lo + PART)
            acc = base[rows, :] + held[half, lo : lo + PART, :].astype(f32)
            rounded = acc.astype(bf16)
            residual_out[rows, :] = rounded
            res = rounded.astype(f32)
            square = square + jnp.sum(res * res, axis=0, keepdims=True)
    factor = lax.rsqrt(square * (1.0 / D) + norm_eps)
    for lo in range(0, D, PART):
        rows = slice(lo, lo + PART)
        res = residual_out[rows, :].astype(f32)
        normed[rows, :] = (res * factor * gain[rows, :].astype(f32)).astype(bf16)
    logits = jnp.dot(router[...], normed[...], preferred_element_type=f32)
    logits = jnp.concatenate(
        [logits[(xh * 4 + z) * 8 : (xh * 4 + z) * 8 + 8] for z in range(4) for xh in range(2)], axis=0
    )
    named = named_of(ids[...])
    raised = jnp.where(named, jnp.exp(logits), 0.0)
    share = raised / jnp.sum(raised, axis=0, keepdims=True)
    high = share.astype(bf16)
    share_out[:EXPERTS, :] = high
    share_out[EXPERTS:, :] = (share - high.astype(f32)).astype(bf16)
    own_out[...] = normed[pl.ds(pl.multiple_of(core * HALF, 32), HALF), :]
    send_out[:HALF, :] = normed[pl.ds(pl.multiple_of((1 - core) * HALF, 32), HALF), :]
    send_out[HALF + 16 :, :] = share_out[...]
    send_out[HALF : HALF + 16, :] = jnp.concatenate(
        [ids[...].astype(f32), jnp.zeros((16 - TOP, TOK), f32)], axis=0
    ).astype(bf16)


def named_of(ids):
    place = lax.broadcasted_iota(jnp.int32, (EXPERTS, TOK), 0)
    expert = ((place >> 3) & 1) * 32 + (place >> 4) * 8 + (place & 7)
    named = expert == ids[0:1, :]
    for k in range(1, TOP):
        named = named | (expert == ids[k : k + 1, :])
    return named


def slots_of(ids, offset):
    named = named_of(ids)
    before = lax.broadcasted_iota(jnp.int32, (TOK, TOK), 0) < lax.broadcasted_iota(
        jnp.int32, (TOK, TOK), 1
    )
    rank = jnp.dot(
        named.astype(f32).astype(bf16), before.astype(f32).astype(bf16), preferred_element_type=f32
    )
    return jnp.where(named, rank + offset, -1.0)


def slot_rows(core, own_ids, other):
    start = (core * CAP).astype(f32)
    other_ids = other[HALF : HALF + 16, :].astype(f32).astype(jnp.int32)
    return slots_of(own_ids[...], start), slots_of(other_ids, CAP - start)


def widened(rows):
    return jnp.concatenate([rows, jnp.zeros((rows.shape[0], WIDE - HALF), rows.dtype)], axis=1)


EXPERT_BLOCK = 16
ROW_BLOCK = EXPERT_BLOCK * PAIR_ROWS


def dispatch_kernel(info, own, other, own_ids, out, slots):
    slots[:, 0:TOK], slots[:, TOK : 2 * TOK] = slot_rows(info[1], own_ids, other)
    tokens = jnp.concatenate([own[...], other[:HALF, :]], axis=1)
    place = lax.broadcasted_iota(jnp.int32, (EXPERT_BLOCK, PAIR_ROWS, 2 * TOK), 1).astype(f32)
    for n in range(EXPERTS // EXPERT_BLOCK):
        block = slots[n * EXPERT_BLOCK : (n + 1) * EXPERT_BLOCK, :]
        hit = block[:, None, :] == place
        pick = jnp.where(hit, 1.0, 0.0).reshape(ROW_BLOCK, 2 * TOK).astype(bf16)
        rows = lax.dot_general(pick, tokens, NT, preferred_element_type=f32).astype(bf16)
        out[n * ROW_BLOCK : (n + 1) * ROW_BLOCK, :] = widened(rows)


def mixing_kernel(info, own_ids, other, own_share, out):
    own_slot, other_slot = slot_rows(info[1], own_ids, other)
    slot = jnp.concatenate([own_slot, other_slot], axis=1).T.astype(bf16)
    parts = jnp.concatenate([own_share[...], other[HALF + 16 :, :]], axis=1).astype(f32)
    high = parts[:EXPERTS].T.astype(bf16)
    rest = parts[EXPERTS:].T.astype(bf16)
    expert = lax.broadcasted_iota(jnp.int32, (EXPERTS, ROWS), 0) * PAIR_ROWS
    offset = lax.broadcasted_iota(jnp.int32, (EXPERTS, ROWS), 1) - expert
    inside = (offset >= 0) & (offset < PAIR_ROWS)
    spread = jnp.where(inside, 1.0, 0.0).astype(bf16)
    place = jnp.sum(jnp.where(inside, offset.astype(f32), 0.0), axis=0, keepdims=True)
    hit = jnp.dot(slot, spread, preferred_element_type=f32) == place
    for part, factor in enumerate((high, rest)):
        wide = jnp.dot(factor, spread, preferred_element_type=f32)
        out[part * 2 * TOK : (part + 1) * 2 * TOK, :] = jnp.where(hit, wide, 0.0).astype(bf16)


def active_kernel(info, own, other, gate_w, up_w, out):
    core = info[1]
    own_rows = pl.ds(pl.multiple_of(core * HALF, 32), HALF)
    other_rows = pl.ds(pl.multiple_of((1 - core) * HALF, 32), HALF)
    x_own = own[:, :HALF]
    x_other = other[:, :HALF]
    gate = jnp.dot(x_own, gate_w[own_rows, :], preferred_element_type=f32)
    gate += jnp.dot(x_other, gate_w[other_rows, :], preferred_element_type=f32)
    up = jnp.dot(x_own, up_w[own_rows, :], preferred_element_type=f32)
    up += jnp.dot(x_other, up_w[other_rows, :], preferred_element_type=f32)
    out[...] = (gate * jax.nn.sigmoid(swiglu_alpha * gate) * (up + 1.0)).astype(bf16)


def down_kernel(starts, info, *refs):
    count = len(starts)
    own, other = refs[:count], refs[count : 2 * count]
    down_w, other_w = refs[2 * count : 2 * count + 2]
    out = refs[-1]
    for n, start in enumerate(starts):
        first = lax.dot_general(own[n][...], down_w[...], NT, preferred_element_type=f32)
        second = lax.dot_general(other[n][...], other_w[...], NT, preferred_element_type=f32)
        both = first.astype(bf16).astype(f32) + second.astype(bf16).astype(f32)
        out[start : start + own[n].shape[0], :] = widened(both.astype(bf16))


MIX_BLOCK = 512


def mix_kernel(factors, rows, own_out, send_out):
    for lo in range(0, WIDE, MIX_BLOCK):
        columns = slice(lo, lo + MIX_BLOCK)
        both = jnp.dot(factors[...], rows[:, columns], preferred_element_type=f32)
        total = both[: 2 * TOK] + both[2 * TOK :]
        own_out[columns, :] = total[:TOK].T
        send_out[columns, :] = total[TOK:].T.astype(bf16)


def final_kernel(info, residual, own, other, out):
    core = info[1]
    for half, ref in ((core, own), (1 - core, other)):
        for lo in range(0, HALF, PART):
            rows = pl.ds(pl.multiple_of(half * HALF + lo, 32), PART)
            mix = ref[lo : lo + PART, :].astype(f32)
            out[rows, :] = (residual[rows, :].astype(f32) + mix).astype(bf16)


def params(mib):
    return pltpu.CompilerParams(vmem_limit_bytes=mib << 20)


def kernel_call(body, outs, operands, with_info=True, scratch=(), mib=40, flops=0, moved=0, remain=()):
    single = not isinstance(outs, list)
    specs = [SMEM_SPEC] * int(with_info) + [VMEM_SPEC] * (len(operands) - int(with_info))
    for n in remain:
        specs[n] = ANY_SPEC
    return pl.pallas_call(
        body,
        out_shape=outs,
        in_specs=specs,
        out_specs=VMEM_SPEC if single else [VMEM_SPEC] * len(outs),
        scratch_shapes=list(scratch),
        compiler_params=params(mib),
        cost_estimate=pl.CostEstimate(flops=flops, bytes_accessed=moved, transcendentals=0),
    )(*operands)


def shape(*dims, dtype=bf16):
    return jax.ShapeDtypeStruct(dims, dtype)


def local(
    hidden_in,
    queries,
    key_heads,
    values,
    doc_lengths,
    out_weight,
    norm_gain,
    router_weight,
    expert_ids,
    gate_weight,
    up_weight,
    down_weight,
):
    upper = lax.axis_index("xh")
    core = lax.axis_index("c")
    depth = lax.axis_index("z")
    info = jnp.stack([upper, core, doc_lengths[0], depth]).astype(jnp.int32)
    swap = [(0, 1), (1, 0)]

    own_w = out_weight.T
    half_w = lax.dynamic_slice_in_dim(own_w, core * HALF, HALF, axis=0)
    q, half_w = lax.optimization_barrier((queries[0], half_w))
    prepared = kernel_call(
        prepare_kernel, shape(4, TOK, 1280), (q, key_heads[0], values[0]), with_info=False
    )
    first_w = lax.ppermute(half_w, ("xh", "xl"), [(0, 3), (3, 0), (1, 2), (2, 1)])
    qkv = lax.all_to_all(prepared, "z", split_axis=0, concat_axis=0, tiled=True).reshape(512, 1280)
    lower = lax.ppermute(qkv[:, 1024:], "xh", [(0, 1)])
    ids = expert_ids[0].T

    def attend(a, qkv):
        return kernel_call(
            functools.partial(attention_kernel, a),
            shape(512, 512),
            (info, qkv, lower),
            scratch=(pltpu.VMEM((2, 1024, 256), bf16),) * 2 + (pltpu.VMEM((512, 256), bf16), DMA(())),
            remain=(2,),
            flops=1000,
            mib=16,
        )

    first_att = attend(0, qkv)
    first_w, first_att, qkv = lax.optimization_barrier((first_w, first_att, qkv))
    second_w = lax.ppermute(first_w, "c", swap)
    second_att = attend(1, qkv)

    plus = [(i, (i + 1) % 4) for i in range(4)]
    minus = [(i, (i + 3) % 4) for i in range(4)]
    weights = (own_w, first_w, second_w)
    half_shape = shape(HALF, TOK)
    half_float = shape(HALF, TOK, dtype=f32)
    far_low, far_high = kernel_call(
        far_kernel,
        [half_shape] * 2,
        (info, first_att, second_att) + weights,
        flops=10**9,
        mib=12,
    )

    far_low = lax.ppermute(far_low, "z", plus)
    far_high = lax.ppermute(far_high, "z", minus)
    up_low, up_high, down_low, down_high, own_part = kernel_call(
        near_kernel,
        [half_float, half_shape, half_shape, half_float, shape(D, TOK, dtype=f32)],
        (info, first_att, second_att) + weights,
        flops=2 * 10**10,
        mib=16,
    )
    high_a = lax.ppermute(up_high, "z", plus)
    low_b = lax.ppermute(down_low, "z", minus)
    relayed = (up_low + far_low.astype(f32)).astype(bf16)
    low_a = lax.ppermute(relayed, "z", plus)
    relayed_high = (down_high + far_high.astype(f32)).astype(bf16)
    high_b = lax.ppermute(relayed_high, "z", minus)

    gate_v, up_v, down_v, send_down = pl.pallas_call(
        stage_kernel,
        out_shape=[pltpu.VMEM((D, FF), bf16)] * 2 + [pltpu.VMEM((HALF, FF), bf16)] * 2,
        in_specs=[SMEM_SPEC] + [HBM_SPEC] * 3 + [ANY_SPEC],
        out_specs=[VMEM_SPEC] * 4,
        scratch_shapes=[DMA((4,))],
        compiler_params=params(16),
    )(info, gate_weight[0], up_weight[0], down_weight[0].T, relayed)
    other_down = lax.ppermute(send_down, "c", swap)
    gain = jnp.broadcast_to(norm_gain[:, None], (D, TOK))
    base = kernel_call(
        presum_kernel,
        shape(D, TOK, dtype=f32),
        (own_part, low_b, high_a, hidden_in[0].T),
        with_info=False,
        mib=12,
    )
    gain, gate_v, up_v, down_v = lax.optimization_barrier((gain, gate_v, up_v, down_v))
    residual, own_half, send_half, share = kernel_call(
        norm_kernel,
        [shape(D, TOK), half_shape, shape(HALF + 16 + 2 * EXPERTS, TOK), shape(2 * EXPERTS, TOK)],
        (info, base, low_a, high_b, gain, router_weight.T, ids),
        scratch=(pltpu.VMEM((D, TOK), bf16), pltpu.VMEM((2, HALF, TOK), bf16), DMA((2,))),
        remain=(2, 3),
        mib=12,
    )
    other_half = lax.ppermute(send_half, "c", swap)

    outgoing = kernel_call(
        dispatch_kernel,
        shape(ROWS, WIDE),
        (info, own_half, other_half, ids),
        scratch=(pltpu.VMEM((EXPERTS, 2 * TOK), f32),),
        mib=16,
    )
    chips = ("z", "xh", "xl", "y")

    def across(rows):
        return lax.all_to_all(
            rows.reshape(EXPERTS, PAIR_ROWS, WIDE), chips, split_axis=0, concat_axis=0, tiled=True
        ).reshape(ROWS, WIDE)

    arrived = across(outgoing)
    arrived, share = lax.optimization_barrier((arrived, share))
    factors = kernel_call(
        mixing_kernel,
        shape(4 * TOK, ROWS),
        (info, ids, other_half, share),
        mib=16,
    )
    own_active, other_active = [], []
    for start, count in STEPS:
        rows = arrived[start : start + count]
        if len(own_active) == 1:
            rows, rows_other = lax.optimization_barrier((rows, rows_other))
        elif own_active:
            rows, rows_other, own_active[0] = lax.optimization_barrier(
                (rows, rows_other, own_active[0])
            )
        rows_other = lax.ppermute(rows, "c", swap)
        if not own_active:
            rows_other, factors = lax.optimization_barrier((rows_other, factors))
        if len(own_active) == 2:
            rows_other, other_active[0] = lax.optimization_barrier((rows_other, other_active[0]))
        active = kernel_call(
            active_kernel,
            shape(count, FF),
            (info, rows, rows_other, gate_v, up_v),
            flops=45 * 10**8,
            mib=20,
        )
        own_active.append(active)
        other_active.append(lax.ppermute(active, "c", swap))

    def down(steps, *buffer):
        picked = [own_active[n] for n in steps] + [other_active[n] for n in steps]
        operands = (info, *picked, down_v, other_down, *buffer)
        return pl.pallas_call(
            functools.partial(down_kernel, [STEPS[n][0] for n in steps]),
            out_shape=shape(ROWS, WIDE),
            in_specs=[SMEM_SPEC] + [VMEM_SPEC] * (len(operands) - 1),
            out_specs=VMEM_SPEC,
            input_output_aliases={len(operands) - 1: 0} if buffer else {},
            compiler_params=params(24),
        )(*operands)

    expert_out = down([2], down([0, 1]))
    own_mix, send_mix = kernel_call(
        mix_kernel,
        [shape(WIDE, TOK, dtype=f32), shape(WIDE, TOK)],
        (factors, across(expert_out)),
        with_info=False,
        mib=24,
    )
    other_mix = lax.ppermute(send_mix, "c", swap)
    layer_out = kernel_call(
        final_kernel, shape(D, TOK), (info, residual, own_mix, other_mix), mib=12
    )
    return layer_out.T[None]


def solution(mesh):
    split_mesh = Mesh(mesh.devices.reshape(2, 4, 2, 4, 2), ("xh", "z", "xl", "y", "c"))
    seq = ("xh", "z")
    doc = ("xl", "y", "c")
    in_specs = (
        P(doc, seq, None),
        P(doc, seq, None),
        P(doc, seq, None),
        P(doc, seq, None),
        P(doc),
        P(seq, None),
        P(),
        P(),
        P(doc, seq, None),
        P(seq + doc, None, None),
        P(seq + doc, None, None),
        P(seq + doc, None, None),
    )
    return jax.shard_map(
        local,
        mesh=split_mesh,
        in_specs=in_specs,
        out_specs=P(doc, seq, None),
        check_vma=False,
    )
```
